512 devices in a mesh: seq: 64 (over z_lo, x, y), dp: 8 (over z_hi, core).
Axes of the slice: x: 4, y: 4, z: 16 (z_hi: 4, z_lo: 4; z = z_hi * 4 + z_lo), core: 2. Of those that a mesh axis runs over, the one named last changes fastest.
Arguments:
- tokens: bfloat16 [16, 64, 128, 1152], P('dp', 'seq'), may hold values from -6 to 6
- modulation: float32 [16, 3, 1152], P('dp'), may hold values from -2.5 to 2.5
- cotangent: bfloat16 [16, 64, 128, 1152], P('dp', 'seq'), may hold values from -13 to 13
- qkv_weight: bfloat16 [1152, 3456], P('seq', 'dp'), may hold values from -0.1875 to 0.1875
- out_weight: bfloat16 [1152, 1152], P('seq', 'dp'), may hold values from -0.1875 to 0.1875
Outputs:
- grad_tokens: bfloat16 [16, 64, 128, 1152], P('dp', 'seq')
- grad_modulation: float32 [16, 2, 1152], P('dp')
The draws below stay inside these ranges and needn't reach their ends.
All inputs are finite; a program needn't handle non-finite values.
Results may differ from the reference program's by a relative error of at most 0.0071.
Values may be sent and summed in bfloat16 or wider, within the bound.
A program may use at most 128 MiB of HBM per device.

```python
import math
import jax
import jax.numpy as jnp
from jax import lax

D = 1152
H = 16
HD = 72
P_SIZE = 128
F = 64
CLIPS = 16


def draw_cotangent(key, part):
    key = jax.random.fold_in(key, 11)
    keys = jax.random.split(key, 1)
    frame_pos = jnp.arange(F, dtype=jnp.float32) / max(F - 1, 1)
    ramp = (0.5 + frame_pos)[None, :, None, None]
    values = jnp.clip(jax.random.normal(keys[0], (CLIPS, F, P_SIZE, D), jnp.float32), -5.0, 5.0) * ramp
    return values.astype(jnp.bfloat16)


def levels(stream_key, dims, pieces, least, top_value):
    def one(dim, shards_of):
        heights = jax.random.uniform(jax.random.fold_in(jax.random.fold_in(stream_key, 6), dim), (shards_of,), jnp.float32, least / len(pieces), top_value / len(pieces))
        return jnp.repeat(jnp.exp(heights), dims[dim] // shards_of).reshape((-1,) + (1,) * (len(dims) - dim - 1))

    factor_of = one(*pieces[0])
    for cut in pieces[1:]:
        factor_of = factor_of * one(*cut)
    return factor_of


def bell_draw(key, extent, spread, bound, shards=(), kind=jnp.bfloat16):
    drawn = jax.random.normal(key, extent, jnp.float32) * spread
    if len(shards) > 0:
        drawn = levels(key, extent, shards, -0.22, 0.18) * drawn
    return jnp.clip(drawn, min=-bound, max=bound).astype(kind)


def setup_inputs(seed: int = 0) -> dict:
    key_of = jax.random.split(jax.random.key(seed), 6)
    tokens = bell_draw(key_of[0], (CLIPS, F, P_SIZE, D), 1.0, 6.0, ((0, 8), (1, 64)))
    modulation = bell_draw(key_of[1], (CLIPS, 3, D), 0.5, 2.5, ((0, 8),), jnp.float32)
    cotangent = draw_cotangent(jax.random.fold_in(key_of[5], 71), 0)
    qkv_weight = bell_draw(key_of[3], (D, 3 * D), D ** -0.5, 0.1875, ((0, 64), (1, 8)))
    out_weight = bell_draw(key_of[4], (D, D), D ** -0.5, 0.1875, ((0, 64), (1, 8)))
    return {"tokens": tokens, "modulation": modulation, "cotangent": cotangent, "qkv_weight": qkv_weight, "out_weight": out_weight}


EPS = 1e-06

def clip_grad(items, qkv_weight, out_weight):
    tokens, modulation, cotangent = items
    frames, patches, model_width = tokens.shape
    tokens_wide = tokens.astype(jnp.float32)
    mean_val = lax.optimization_barrier(jnp.mean(tokens_wide, axis=-1, keepdims=True))
    centred = tokens_wide - mean_val
    inv_std = lax.rsqrt(lax.optimization_barrier(jnp.mean(centred * centred, axis=-1, keepdims=True)) + EPS)
    normed = centred * inv_std
    mod_shift = modulation[0]
    mod_scale = modulation[1]
    mod_gate = modulation[2]
    hidden = (normed * (1.0 + mod_scale) + mod_shift).astype(jnp.bfloat16)
    row_count = frames * patches
    projected = jnp.dot(hidden.reshape(row_count, model_width), qkv_weight, preferred_element_type=jnp.float32).astype(jnp.bfloat16)
    split = projected.reshape(frames, patches, 3, H, HD).astype(jnp.float32)
    query = split[:, :, 0]
    keys = split[:, :, 1]
    values = split[:, :, 2]
    gated_grad = (cotangent.astype(jnp.float32) * mod_gate).astype(jnp.bfloat16)
    grad_attn = jnp.dot(gated_grad.reshape(row_count, model_width), out_weight.T, preferred_element_type=jnp.float32).astype(jnp.bfloat16)
    grad_heads = grad_attn.reshape(frames, patches, H, HD).astype(jnp.float32)
    score_scale = 1.0 / math.sqrt(HD)
    scores = jnp.einsum('fphe,gphe->phfg', query, keys) * score_scale
    exp_scores = jnp.exp(scores)
    attn_probs = exp_scores / lax.optimization_barrier(jnp.sum(exp_scores, axis=-1, keepdims=True))
    probs_low = attn_probs.astype(jnp.bfloat16).astype(jnp.float32)
    grad_probs = jnp.einsum('fphe,gphe->phfg', grad_heads, values)
    inner = lax.optimization_barrier(jnp.sum(attn_probs * grad_probs, axis=-1, keepdims=True))
    grad_scores = (attn_probs * (grad_probs - inner) * score_scale).astype(jnp.bfloat16).astype(jnp.float32)
    grad_query = jnp.einsum('phfg,gphe->fphe', grad_scores, keys)
    grad_keys = jnp.einsum('phfg,fphe->gphe', grad_scores, query)
    grad_values = jnp.einsum('phfg,fphe->gphe', probs_low, grad_heads)
    grad_proj = jnp.stack([grad_query, grad_keys, grad_values], axis=2).astype(jnp.bfloat16)
    grad_proj = grad_proj.reshape(row_count, 3 * model_width)
    grad_hidden = jnp.dot(grad_proj, qkv_weight.T, preferred_element_type=jnp.float32).reshape(frames, patches, model_width)
    grad_shift = lax.optimization_barrier(jnp.sum(grad_hidden, axis=(0, 1)))
    grad_scale = lax.optimization_barrier(jnp.sum(grad_hidden * normed, axis=(0, 1)))
    grad_normed = grad_hidden * (1.0 + mod_scale)
    mean_grad = lax.optimization_barrier(jnp.mean(grad_normed, axis=-1, keepdims=True))
    mean_cross = lax.optimization_barrier(jnp.mean(grad_normed * normed, axis=-1, keepdims=True))
    grad_tokens = cotangent.astype(jnp.float32) + inv_std * (grad_normed - mean_grad - normed * mean_cross)
    return (grad_tokens.astype(jnp.bfloat16), jnp.stack([grad_shift, grad_scale], axis=0))

def reference(tokens, modulation, cotangent, qkv_weight, out_weight):
    grad_tokens, grad_modulation = lax.map(lambda items: clip_grad(items, qkv_weight, out_weight), (tokens, modulation, cotangent))
    return (grad_tokens, grad_modulation)
```

```python
import functools
import math

import jax
import jax.numpy as jnp
import numpy as np
from jax import lax
from jax.experimental import pallas as pl
from jax.experimental.pallas import tpu as pltpu
from jax.sharding import PartitionSpec as P

D = 1152
H = 16
HD = 72
EPS = 1e-06
MESH = pl.DeviceIdType.MESH
BF = jnp.bfloat16
F32 = jnp.float32
RHS_T = (((1,), (1,)), ((), ()))
LHS_T = (((0,), (0,)), ((), ()))


def place_tables():
    tables = np.zeros((2, D, D), np.float32)
    feature = np.arange(D)
    zl, rest = feature // 288, feature % 288
    x, rest = rest // 72, rest % 72
    y, i = rest // 18, rest % 18
    tables[0, feature, y * 288 + x * 72 + zl * 18 + i] = 1
    tables[1, feature, x * 288 + y * 72 + zl * 18 + i] = 1
    return tables


def dot(a, b, dims=(((1,), (0,)), ((), ()))):
    return lax.dot_general(a, b, dims, preferred_element_type=F32)


def iota(shape, dim):
    return lax.broadcasted_iota(jnp.int32, shape, dim)


def pick(source_row, n=256, m=256):
    return (source_row(iota((n, m), 0)) == iota((n, m), 1)).astype(F32).astype(BF)


def kernel(
    tok_ref, mod_ref, cot_ref, wq_ref, wo_ref, table_hbm,
    out_ref, outm_ref,
    sa, ra, sb, rb, z, h, g1, w, table, hid, gated, normed, inv, pr, acc, gp, rr, rr2, ms, mr, ms2, mr2,
    table_sem, zh_s, zh_r, zl_s, zl_r, zc_s, zc_r, p1_s, p1_r, p2_s, p2_r, pc_s, pc_r,
    a_s, a_r, b_s, b_r, c_s, c_r, e_s, e_r, cm_s, cm_r, em_s, em_r,
):
    s, q = lax.axis_index("seq"), lax.axis_index("dp")
    y, x, zl = lax.rem(s, 4), lax.rem(s // 4, 4), s // 16
    zh, c = q // 2, lax.rem(q, 2)
    xy = x * 4 + y
    zfull = zh * 4 + zl
    m4 = lambda v: lax.rem(v + 8, 4)

    def dev(x_, y_, z_, c_):
        return ((lax.rem(z_, 4) * 4 + x_) * 4 + y_, (z_ // 4) * 2 + c_)

    def at_xy(k):
        return dev(m4(x + k // 4), m4(y + lax.rem(k, 4)), zfull, c)

    def at_zl(k):
        return dev(x, y, zh * 4 + m4(zl + k), c)

    def at_zh(k):
        return dev(x, y, m4(zh + k) * 4 + zl, c)

    def at_ring(k):
        return dev(x, y, lax.rem(zfull + k + 16, 16), c)

    other = dev(x, y, zfull, 1 - c)

    def copy(src, dst, ss, rs, to):
        return pltpu.make_async_remote_copy(
            src_ref=src, dst_ref=dst, send_sem=ss, recv_sem=rs, device_id=to, device_id_type=MESH
        )

    tables_in = pltpu.make_async_copy(table_hbm, table, table_sem)
    tables_in.start()

    wide = jnp.concatenate(
        [wq_ref[...].astype(F32), wo_ref[...].astype(F32), jnp.zeros((18, 64), F32)], axis=1
    )
    z[c, zl, zh] = jnp.concatenate([wide, jnp.zeros((14, 640), F32)], axis=0).astype(BF)

    barrier = pltpu.get_barrier_semaphore()

    def greet(to):
        pl.semaphore_signal(barrier, inc=1, device_id=to, device_id_type=MESH)

    greet(other)
    for k in (1, 2, 3):
        greet(at_zh(k))
        greet(at_zl(k))
    for k in (1, -1, 2, -2):
        greet(at_ring(k))

    @pl.loop(1, 16)
    def _(k):
        greet(at_xy(k))

    pl.semaphore_wait(barrier, 26)

    zh_copies = [copy(z.at[c, zl, zh], z.at[c, zl, zh], zh_s.at[k], zh_r.at[k], at_zh(k)) for k in (1, 2, 3)]
    zh_copies = dict(zip((1, 2, 3), zh_copies))
    for k in (1, 2, 3):
        zh_copies[k].start()

    def a_copy(n, k):
        return copy(sa.at[n, lax.rem(x + k // 4, 4) * 4 + lax.rem(y + lax.rem(k, 4), 4)], ra.at[n, xy],
                    a_s.at[n, k], a_r.at[n, k], at_xy(k))

    to_plane = pick(lambda o: ((o >> 3) & 1) * 128 + (o >> 4) * 8 + (o & 7))
    for n, source in enumerate((tok_ref, cot_ref)):
        rows = source[...].reshape(256, D)
        sa[n] = dot(to_plane, rows).astype(BF).reshape(16, 16, D)

        @pl.loop(1, 16)
        def _(k, n=n):
            a_copy(n, k).start()

        ra[n, xy] = sa[n, xy]

    for k in (1, 2, 3):
        zh_copies[k].wait()

    zl_copies = [copy(z.at[c, zl], z.at[c, zl], zl_s.at[n], zl_r.at[n], at_ring(k)) for n, k in enumerate((1, -1, 2))]
    for cp in zl_copies:
        cp.start()

    def b_copy(n, k):
        return copy(sb.at[n, m4(zl + k)], rb.at[n, zl], b_s.at[n, k], b_r.at[n, k], at_zl(k))

    to_line = pick(lambda o: ((o >> 2) & 15) * 16 + ((o >> 1) & 1) * 8 + (o >> 6) * 2 + (o & 1))

    def second_step(n):
        @pl.loop(1, 16)
        def _(k):
            a_copy(n, k).wait()

        sb[n] = dot(to_line, ra[n].reshape(256, D)).astype(BF).reshape(4, 64, D)
        for k in (1, 2, 3):
            b_copy(n, k).start()
        rb[n, zl] = sb[n, zl]

    for cp in zl_copies:
        cp.wait()
    zc = copy(z.at[c], z.at[c], zc_s, zc_r, other)
    zc.start()
    second_step(0)
    zc.wait()

    def block(d):
        return jnp.concatenate([z[d % 2, k, d // 2][0:18, :].astype(F32) for k in range(4)], axis=0)

    blocks = [block(d) for d in range(8)]
    full = jnp.concatenate([b[:, :432] for b in blocks] + [b[:, 432:576] for b in blocks], axis=1)
    full = jnp.concatenate([full, jnp.zeros((8, 4 * D), F32)], axis=0).astype(BF)
    for k in range(4):
        h[k] = full[:, k * D:(k + 1) * D]

    p1_copies = []
    for k in (1, 2, 3):
        p1_copies.append(copy(h.at[2 * c], g1.at[0, x], p1_s.at[0, k], p1_r.at[0, k], dev(m4(x + k), y, zfull, c)))
        p1_copies.append(copy(h.at[2 * c + 1], g1.at[1, y], p1_s.at[1, k], p1_r.at[1, k], dev(x, m4(y + k), zfull, c)))
    for cp in p1_copies:
        cp.start()
    g1[0, x] = h[2 * c]
    g1[1, y] = h[2 * c + 1]

    second_step(1)
    for cp in p1_copies:
        cp.wait()

    squeeze = pick(
        lambda o: o + 8 * ((o >= 72).astype(jnp.int32) + (o >= 144).astype(jnp.int32) + (o >= 216).astype(jnp.int32)),
        288, 320,
    )
    own = (y, x)
    halves = (pl.ds(0, 144), pl.ds(144, 144))
    p2, pc = [], []
    for a in range(2):
        quarter = 2 * c + a
        w[quarter, own[a]] = dot(squeeze, g1[a].reshape(320, D)).astype(BF)
        right = dev(x, m4(y + 1), zfull, c) if a == 0 else dev(m4(x + 1), y, zfull, c)
        left = dev(x, m4(y - 1), zfull, c) if a == 0 else dev(m4(x - 1), y, zfull, c)

        def move(n, slot, half, to, a=a, quarter=quarter):
            ref = w.at[quarter, slot, half]
            return copy(ref, ref, p2_s.at[a, n], p2_r.at[a, n], to)

        me, lo, hi = own[a], m4(own[a] - 1), m4(own[a] + 1)
        p2.append([
            move(0, me, halves[0], right), move(1, me, halves[1], left),
            move(2, me, halves[1], right), move(3, me, halves[0], left),
            move(4, lo, halves[0], right), move(5, hi, halves[1], left),
        ])
        for n in range(4):
            p2[a][n].start()

        def across(n, slot, a=a, quarter=quarter):
            ref = w.at[quarter, slot]
            return copy(ref, ref, pc_s.at[a, n], pc_r.at[a, n], other)

        pc.append([across(0, me), across(1, lo), across(2, hi), across(3, m4(me + 2))])
        pc[a][0].start()

    for n in (0, 1):
        for k in (1, 2, 3):
            b_copy(n, k).wait()
    tables_in.wait()

    def clip_of(rows_shape):
        return ((iota(rows_shape, 0) >> 1) & 1) == 1

    def norm_rows(i):
        rows = pl.ds(pl.multiple_of(i * 32, 32), 32)
        tile = rb.at[0, i // 2][pl.ds(pl.multiple_of(lax.rem(i, 2) * 32, 32), 32), :].astype(F32)
        cot = rb.at[1, i // 2][pl.ds(pl.multiple_of(lax.rem(i, 2) * 32, 32), 32), :].astype(F32)
        mean = jnp.sum(tile, axis=1, keepdims=True) * (1.0 / D)
        centred = tile - mean
        inv_std = lax.rsqrt(jnp.sum(centred * centred, axis=1, keepdims=True) * (1.0 / D) + EPS)
        nrm = centred * inv_std
        normed[rows, :] = nrm
        inv[rows, :] = jnp.broadcast_to(inv_std, (32, 128))
        second = clip_of((32, D))
        shift = jnp.where(second, mod_ref[1, 0:1, :], mod_ref[0, 0:1, :])
        scale = jnp.where(second, mod_ref[1, 1:2, :], mod_ref[0, 1:2, :])
        gate = jnp.where(second, mod_ref[1, 2:3, :], mod_ref[0, 2:3, :])
        hid[0, rows, :] = (nrm * (1.0 + scale) + shift).astype(BF)
        gated[rows, :] = (cot * gate).astype(BF)

    pl.loop(0, 8)(norm_rows)
    hidden = hid[0]
    hid[1] = dot(hidden, table[1]).astype(BF)
    hid[0] = dot(hidden, table[0]).astype(BF)

    for a in range(2):
        p2[a][0].wait()
        p2[a][4].start()
        p2[a][1].wait()
        p2[a][5].start()
    for a in range(2):
        p2[a][2].wait()
        pc[a][1].start()
        p2[a][3].wait()
        pc[a][2].start()
    for a in range(2):
        p2[a][4].wait()
        p2[a][5].wait()
        pc[a][3].start()
    for a in range(2):
        for cp in pc[a]:
            cp.wait()

    def project(i):
        quarter = i // 3
        cols = pl.ds(pl.multiple_of(lax.rem(i, 3) * 384, 128), 384)
        pr[quarter, :, cols] = dot(hid[lax.rem(quarter, 2)], w[quarter, :, :, cols].reshape(D, 384)).astype(BF)

    pl.loop(0, 9)(project)
    ga = dot(gated[...], w[3].reshape(D, D), RHS_T).astype(BF)
    pr[3] = dot(ga, table[1], RHS_T).astype(BF)

    acc[...] = jnp.zeros_like(acc)
    score_scale = 1.0 / math.sqrt(HD)
    same = (iota((256, 256), 0) & 3) == (iota((256, 256), 1) & 3)

    def head(i):
        first = jnp.minimum((i * HD) // 128, 7)
        cols = pl.ds(pl.multiple_of(first * 128, 128), 256)
        lane = iota((256, 256), 1) - (i * HD - first * 128)
        inside = (lane >= 0) & (lane < HD)
        zero = jnp.zeros((256, 256), BF)
        query = jnp.where(inside, pr[0, :, cols], zero)
        keys = jnp.where(inside, pr[1, :, cols], zero)
        values = pr[2, :, cols]
        grad = jnp.where(inside, pr[3, :, cols], zero)
        scores = dot(keys, query, RHS_T) * score_scale
        e = jnp.exp(jnp.where(same, scores, -jnp.inf))
        probs = e / jnp.sum(e, axis=0, keepdims=True)
        grad_probs = dot(values, grad, RHS_T)
        inner = jnp.sum(probs * grad_probs, axis=0, keepdims=True)
        grad_scores = (probs * (grad_probs - inner) * score_scale).astype(BF)
        acc[0, :, cols] += dot(grad_scores, keys, LHS_T)
        acc[1, :, cols] += dot(grad_scores, query)
        acc[2, :, cols] += dot(probs.astype(BF), grad)

    pl.loop(0, H)(head)
    for k in range(3):
        gp[k] = acc[k].astype(BF)

    gha = dot(gp[0], w[0].reshape(D, D), RHS_T) + dot(gp[2], w[2].reshape(D, D), RHS_T)
    ghb = dot(gp[1], w[1].reshape(D, D), RHS_T)
    acc[0] = gha
    acc[1] = ghb
    for k in range(2):
        top = acc[k].astype(BF)
        gp[0] = top
        gp[1] = (acc[k] - top.astype(F32)).astype(BF)
        part = dot(gp[0], table[k], RHS_T) + dot(gp[1], table[k], RHS_T)
        if k == 0:
            acc[2] = part
        else:
            acc[2] += part

    ms[...] = jnp.zeros_like(ms)

    def norm_back(i):
        rows = pl.ds(pl.multiple_of(i * 32, 32), 32)
        inside = pl.ds(pl.multiple_of(lax.rem(i, 2) * 32, 32), 32)
        gh = acc[2, rows, :]
        nrm = normed[rows, :]
        second = clip_of((32, D))
        zero = jnp.zeros_like(gh)
        cross = gh * nrm
        ms[0:1, :] += jnp.sum(jnp.where(second, zero, gh), axis=0, keepdims=True)
        ms[1:2, :] += jnp.sum(jnp.where(second, zero, cross), axis=0, keepdims=True)
        ms[2:3, :] += jnp.sum(jnp.where(second, gh, zero), axis=0, keepdims=True)
        ms[3:4, :] += jnp.sum(jnp.where(second, cross, zero), axis=0, keepdims=True)
        gn = gh * (1.0 + jnp.where(second, mod_ref[1, 1:2, :], mod_ref[0, 1:2, :]))
        mean_grad = jnp.sum(gn, axis=1, keepdims=True) * (1.0 / D)
        mean_cross = jnp.sum(gn * nrm, axis=1, keepdims=True) * (1.0 / D)
        cot = rb.at[1, i // 2][inside, :].astype(F32)
        gt = cot + inv[rows, 0:1] * (gn - mean_grad - nrm * mean_cross)
        rr.at[0, i // 2][inside, :] = gt.astype(BF)

    pl.loop(0, 8)(norm_back)

    back = {}
    for k in (1, 2, 3):
        back[k] = copy(rr.at[0, m4(zl + k)], rr.at[1, zl], c_s.at[k], c_r.at[k], at_zl(k))
        back[k].start()
    mod_back = {}
    for k in (1, 2, 3):
        mod_back[k] = copy(ms, mr.at[zl], cm_s.at[k], cm_r.at[k], at_zl(k))
        mod_back[k].start()
    rr[1, zl] = rr[0, zl]
    mr[zl] = ms[...]
    for k in (1, 2, 3):
        mod_back[k].wait()
    ms2[...] = ((mr[0] + mr[1]) + mr[2]) + mr[3]

    def em_copy(k):
        return copy(ms2, mr2.at[xy], em_s.at[k], em_r.at[k], at_xy(k))

    @pl.loop(1, 16)
    def _(k):
        em_copy(k).start()

    mr2[xy] = ms2[...]
    for k in (1, 2, 3):
        back[k].wait()

    from_line = pick(lambda o: ((o >> 1) & 3) * 64 + (o >> 4) * 4 + ((o >> 3) & 1) * 2 + (o & 1))
    rr2[0] = dot(from_line, rr[1].reshape(256, D)).astype(BF).reshape(16, 16, D)

    def e_copy(k):
        return copy(rr2.at[0, lax.rem(x + k // 4, 4) * 4 + lax.rem(y + lax.rem(k, 4), 4)], rr2.at[1, xy],
                    e_s.at[k], e_r.at[k], at_xy(k))

    @pl.loop(1, 16)
    def _(k):
        e_copy(k).start()

    rr2[1, xy] = rr2[0, xy]

    @pl.loop(1, 16)
    def _(k):
        em_copy(k).wait()

    total = mr2[0]
    for k in range(1, 16):
        total = total + mr2[k]
    outm_ref[0] = total[0:2]
    outm_ref[1] = total[2:4]

    @pl.loop(1, 16)
    def _(k):
        e_copy(k).wait()

    from_plane = pick(lambda o: ((o >> 3) & 15) * 16 + (o >> 7) * 8 + (o & 7))
    out_ref[...] = dot(from_plane, rr2[1].reshape(256, D)).astype(BF).reshape(2, 1, 128, D)


def local(tokens, modulation, cotangent, qkv_weight, out_weight):
    tables = jnp.asarray(place_tables(), BF)
    vmem = pl.BlockSpec(memory_space=pltpu.VMEM)
    dma = pltpu.SemaphoreType.DMA
    return pl.pallas_call(
        kernel,
        out_shape=(
            jax.ShapeDtypeStruct((2, 1, 128, D), BF),
            jax.ShapeDtypeStruct((2, 2, D), F32),
        ),
        in_specs=[vmem] * 5 + [pl.BlockSpec(memory_space=pl.ANY)],
        out_specs=(vmem, vmem),
        scratch_shapes=[
            pltpu.VMEM((2, 16, 16, D), BF),
            pltpu.VMEM((2, 16, 16, D), BF),
            pltpu.VMEM((2, 4, 64, D), BF),
            pltpu.VMEM((2, 4, 64, D), BF),
            pltpu.VMEM((2, 4, 4, 32, 640), BF),
            pltpu.VMEM((4, 80, D), BF),
            pltpu.VMEM((2, 4, 80, D), BF),
            pltpu.VMEM((4, 4, 288, D), BF),
            pltpu.VMEM((2, D, D), BF),
            pltpu.VMEM((2, 256, D), BF),
            pltpu.VMEM((256, D), BF),
            pltpu.VMEM((256, D), F32),
            pltpu.VMEM((256, 128), F32),
            pltpu.VMEM((4, 256, D), BF),
            pltpu.VMEM((3, 256, D), F32),
            pltpu.VMEM((3, 256, D), BF),
            pltpu.VMEM((2, 4, 64, D), BF),
            pltpu.VMEM((2, 16, 16, D), BF),
            pltpu.VMEM((8, D), F32),
            pltpu.VMEM((4, 8, D), F32),
            pltpu.VMEM((8, D), F32),
            pltpu.VMEM((16, 8, D), F32),
            dma,
            dma((4,)), dma((4,)), dma((3,)), dma((3,)), dma, dma,
            dma((2, 4)), dma((2, 4)), dma((2, 6)), dma((2, 6)), dma((2, 4)), dma((2, 4)),
            dma((2, 16)), dma((2, 16)), dma((2, 4)), dma((2, 4)),
            dma((4,)), dma((4,)), dma((16,)), dma((16,)),
            dma((4,)), dma((4,)), dma((16,)), dma((16,)),
        ],
        compiler_params=pltpu.CompilerParams(
            collective_id=0, has_side_effects=True, vmem_limit_bytes=60 * 1024 * 1024
        ),
        name="sublayer_backward",
    )(tokens, modulation, cotangent, qkv_weight, out_weight, tables)


def solution(mesh):
    in_specs = (
        P("dp", "seq", None, None),
        P("dp", None, None),
        P("dp", "seq", None, None),
        P("seq", "dp"),
        P("seq", "dp"),
    )
    out_specs = (P("dp", "seq", None, None), P("dp", None, None))
    return jax.shard_map(local, mesh=mesh, in_specs=in_specs, out_specs=out_specs, check_vma=False)
```

```python
import functools
import math

import jax
import jax.numpy as jnp
import numpy as np
from jax import lax
from jax.experimental import pallas as pl
from jax.experimental.pallas import tpu as pltpu
from jax.sharding import PartitionSpec as P

D = 1152
H = 16
HD = 72
EPS = 1e-06
MESH = pl.DeviceIdType.MESH
BF = jnp.bfloat16
F32 = jnp.float32
RHS_T = (((1,), (1,)), ((), ()))
LHS_T = (((0,), (0,)), ((), ()))


MAIN, TAIL = 1024, 256


def place_table():
    table = np.zeros((D, MAIN + 2 * TAIL), np.float32)
    for feature in range(D):
        zl, rest = divmod(feature, 288)
        position, i = divmod(rest, 18)
        t = zl * 18 + i
        if t < 64:
            table[feature, position * 64 + t] = 1
        else:
            table[feature, MAIN + position * 16 + t - 64] = 1
            table[feature, MAIN + TAIL + position * 16 + 8 + t - 64] = 1
    return table


def dot(a, b, dims=(((1,), (0,)), ((), ()))):
    return lax.dot_general(a, b, dims, preferred_element_type=F32)


def iota(shape, dim):
    return lax.broadcasted_iota(jnp.int32, shape, dim)


def pick(source_row, n=256, m=256):
    return (source_row(iota((n, m), 0)) == iota((n, m), 1)).astype(F32).astype(BF)


def kernel(
    tok_hbm, mod_hbm, cot_hbm, wq_hbm, wo_hbm, table_hbm,
    out_hbm, outm_ref,
    raw, mod_ref, wq_ref, wo_ref,
    sa, ra, sb, rb, z, x80, x64, table, hid, hidp, gated, normed, inv, pr, acc, gp, gh_low, rr, rr2, sums, ms, mr,
    in_sem, out_sem, zh_s, zh_r, zl_s, zl_r, zc_s, zc_r, w_s, w_r, wc_s, wc_r,
    a_s, a_r, b_s, b_r, c_s, c_r, e_s, e_r, m_s, m_r,
):
    s, q = lax.axis_index("seq"), lax.axis_index("dp")
    y, x, zl = lax.rem(s, 4), lax.rem(s // 4, 4), s // 16
    zh, c = q // 2, lax.rem(q, 2)
    xy = x * 4 + y
    zfull = zh * 4 + zl

    def m4(v):
        return lax.rem(v + 8, 4)

    def dev(x_, y_, z_, c_):
        return ((lax.rem(z_, 4) * 4 + x_) * 4 + y_, (z_ // 4) * 2 + c_)

    def at_xy(k):
        return dev(m4(x + k // 4), m4(y + lax.rem(k, 4)), zfull, c)

    def at_zl(k):
        return dev(x, y, zh * 4 + m4(zl + k), c)

    def at_zh(k):
        return dev(x, y, m4(zh + k) * 4 + zl, c)

    def at_ring(k):
        return dev(x, y, lax.rem(zfull + k + 16, 16), c)

    other = dev(x, y, zfull, 1 - c)

    def copy(src, dst, ss, rs, to):
        return pltpu.make_async_remote_copy(
            src_ref=src, dst_ref=dst, send_sem=ss, recv_sem=rs, device_id=to, device_id_type=MESH
        )

    loads = [
        pltpu.make_async_copy(src, dst, in_sem.at[n])
        for n, (src, dst) in enumerate((
            (wq_hbm, wq_ref), (wo_hbm, wo_ref), (tok_hbm, raw.at[0]), (cot_hbm, raw.at[1]),
            (mod_hbm, mod_ref), (table_hbm, table),
        ))
    ]
    for load in loads:
        load.start()

    barrier = pltpu.get_barrier_semaphore()

    def greet(to):
        pl.semaphore_signal(barrier, inc=1, device_id=to, device_id_type=MESH)

    for k in (1, 2, 3):
        greet(at_zh(k))
        greet(at_zl(k))
    for k in (1, -1, 2, -2):
        greet(at_ring(k))
    greet(other)

    @pl.loop(1, 16)
    def _(k):
        greet(at_xy(k))

    loads[0].wait()
    loads[1].wait()
    wide = jnp.concatenate(
        [wq_ref[...].astype(F32), wo_ref[...].astype(F32), jnp.zeros((18, 64), F32)], axis=1
    )
    ends = [wide[16 + j:17 + j, 128 * m:128 * m + 128] for j in range(2) for m in range(5)]
    ends = jnp.concatenate(ends + [jnp.zeros((6, 128), F32)], axis=0)
    z[c, zl, zh] = jnp.concatenate([wide[:16], ends], axis=1).astype(BF)

    to_plane = pick(lambda o: ((o >> 3) & 1) * 128 + (o >> 4) * 8 + (o & 7))

    def first_order(n):
        loads[2 + n].wait()
        sa[n] = dot(to_plane, raw[n].reshape(256, D)).astype(BF).reshape(16, 16, D)

    first_order(0)
    pl.semaphore_wait(barrier, 26)

    def zh_copy(k):
        ref = z.at[c, zl, zh]
        return copy(ref, ref, zh_s.at[k], zh_r.at[k], at_zh(k))

    ring = (1, -1, 2)

    def zl_copy(n, group):
        ref = z.at[c, zl, group]
        return copy(ref, ref, zl_s.at[n, group], zl_r.at[n, group], at_ring(ring[n]))

    def zl_arrived(n, group):
        ref = z.at[c, m4(zl - ring[n]), group]
        copy(ref, ref, zl_s.at[n, group], zl_r.at[n, group], at_ring(ring[n])).wait_recv()

    def zc_copy(line, n):
        ref = z.at[c, line]
        return copy(ref, ref, zc_s.at[n], zc_r.at[n], other)

    for k in (2, 1, 3):
        zh_copy(k).start()
    for n in range(3):
        zl_copy(n, zh).start()

    def a_copy(n, k):
        return copy(sa.at[n, m4(x + k // 4) * 4 + m4(y + lax.rem(k, 4))], ra.at[n, xy],
                    a_s.at[n, k], a_r.at[n, k], at_xy(k))

    def a_send(n):
        @pl.loop(1, 16)
        def _(k):
            a_copy(n, k).start()

        ra[n, xy] = sa[n, xy]

    a_send(0)
    first_order(1)
    a_send(1)

    for k in (1, 3, 2):
        zh_copy(k).wait_recv()
        for n in range(3):
            zl_copy(n, m4(zh - k)).start()
    zc_copy(zl, 0).start()

    def b_copy(n, k):
        return copy(sb.at[n, m4(zl + k)], rb.at[n, zl], b_s.at[n, k], b_r.at[n, k], at_zl(k))

    to_line = pick(lambda o: ((o >> 2) & 15) * 16 + ((o >> 1) & 1) * 8 + (o >> 6) * 2 + (o & 1))

    def second_step(n):
        @pl.loop(1, 16)
        def _(k):
            a_copy(n, k).wait()

        sb[n] = dot(to_line, ra[n].reshape(256, D)).astype(BF).reshape(4, 64, D)
        for k in (2, 1, 3):
            b_copy(n, k).start()
        rb[n, zl] = sb[n, zl]

    for n in range(3):
        for k in range(4):
            zl_arrived(n, m4(zh - k))
        zc_copy(m4(zl - ring[n]), 1 + n).start()
    second_step(0)
    for n in range(4):
        ref = z.at[1 - c, m4(zl - (0, 1, -1, 2)[n])]
        copy(ref, ref, zc_s.at[n], zc_r.at[n], other).wait_recv()

    def block(d):
        parts = []
        for k in range(4):
            stored = z[d % 2, k, d // 2].astype(F32)
            parts.append(stored[:, :640])
            for j in range(2):
                parts.append(jnp.concatenate(
                    [stored[5 * j + m:5 * j + m + 1, 640:768] for m in range(5)], axis=1
                ))
        return jnp.concatenate(parts, axis=0)

    blocks = [block(d) for d in range(8)]
    full = jnp.concatenate([b[:, :432] for b in blocks] + [b[:, 432:576] for b in blocks], axis=1)
    quarters = [full[:, k * D:(k + 1) * D] for k in range(4)]
    x80[0, xy, 0:64, :] = quarters[0][:64].astype(BF)
    x80[0, xy, 64:80, :] = jnp.concatenate([quarters[0][64:], quarters[1][64:]], axis=0).astype(BF)
    x64[0, xy] = quarters[1][:64].astype(BF)
    x80[1, xy, 0:64, :] = quarters[3][:64].astype(BF)
    x80[1, xy, 64:80, :] = jnp.concatenate([quarters[2][64:], quarters[3][64:]], axis=0).astype(BF)
    x64[1, xy] = quarters[2][:64].astype(BF)

    stores = (x80, x64)
    first_axis = (((1 - c), c), (c, (1 - c)))

    def shifted(st, i, j):
        fx, fy = first_axis[st]
        return m4(x + i * fx + j * fy), m4(y + i * fy + j * fx)

    def position(st, i, j):
        px, py = shifted(st, i, j)
        return px * 4 + py

    sent = []

    def w_send(st, i, j, to_i, to_j):
        ref = stores[st].at[c, position(st, i, j)]
        px, py = shifted(st, to_i, to_j)
        index = ((i - to_i) % 4) * 4 + (j - to_j) % 4
        cp = copy(ref, ref, w_s.at[st, index], w_r.at[st, index], dev(px, py, zfull, c))
        cp.start()
        sent.append(cp)

    def w_arrived(st, i, j):
        ref = stores[st].at[c, position(st, i, j)]
        index = i * 4 + j
        copy(ref, ref, w_s.at[st, index], w_r.at[st, index], other).wait_recv()
        cp = copy(ref, ref, wc_s.at[st, index], wc_r.at[st, index], other)
        cp.start()
        sent.append(cp)

    def w_both_ways(st, i):
        w_send(st, i, 0, 0, 1)
        w_send(st, i, 0, 0, -1)

    def w_sides(st, i):
        w_arrived(st, i, 3)
        if i in (0, 2):
            w_send(st, i, 3, 0, 1)
        w_arrived(st, i, 1)
        if i in (1, 3):
            w_send(st, i, 1, 0, -1)

    for st in range(2):
        for i in (1, -1, 2):
            w_send(st, 0, 0, i, 0)
        w_both_ways(st, 0)

    second_step(1)
    for i in (1, 3):
        for st in range(2):
            w_arrived(st, i, 0)
            w_both_ways(st, i)
    for st in range(2):
        w_sides(st, 0)
    for st in range(2):
        w_arrived(st, 2, 0)
        w_both_ways(st, 2)

    for n in (0, 1):
        for k in (1, 2, 3):
            b_copy(n, k).wait()
    loads[4].wait()
    loads[5].wait()

    def clip_of(rows_shape):
        return ((iota(rows_shape, 0) >> 1) & 1) == 1

    def norm_rows(i):
        rows = pl.ds(pl.multiple_of(i * 32, 32), 32)
        tile = rb.at[0, i // 2][pl.ds(pl.multiple_of(lax.rem(i, 2) * 32, 32), 32), :].astype(F32)
        cot = rb.at[1, i // 2][pl.ds(pl.multiple_of(lax.rem(i, 2) * 32, 32), 32), :].astype(F32)
        mean = jnp.sum(tile, axis=1, keepdims=True) * (1.0 / D)
        centred = tile - mean
        inv_std = lax.rsqrt(jnp.sum(centred * centred, axis=1, keepdims=True) * (1.0 / D) + EPS)
        nrm = centred * inv_std
        normed[rows, :] = nrm
        inv[rows, :] = jnp.broadcast_to(inv_std, (32, 128))
        second = clip_of((32, D))
        shift = jnp.where(second, mod_ref[0, 1:2, :], mod_ref[0, 0:1, :])
        scale = jnp.where(second, mod_ref[1, 1:2, :], mod_ref[1, 0:1, :])
        gate = jnp.where(second, mod_ref[2, 1:2, :], mod_ref[2, 0:1, :])
        hid[rows, :] = (nrm * (1.0 + scale) + shift).astype(BF)
        gated[rows, :] = (cot * gate).astype(BF)

    pl.loop(0, 8)(norm_rows)
    hidp[...] = dot(hid[...], table[...]).astype(BF)

    for i in (1, 3, 2):
        for st in range(2):
            w_sides(st, i)
    for i in range(4):
        for st in range(2):
            w_arrived(st, i, 2)
    for k in range(1, 16):
        for st in range(2):
            ref = stores[st].at[1 - c, position(1 - st, k // 4, k % 4)]
            copy(ref, ref, wc_s.at[st, k], wc_r.at[st, k], other).wait_recv()
    for cp in sent:
        cp.wait_send()
    for k in (1, 2, 3):
        zh_copy(k).wait_send()
    for n in range(3):
        for k in range(4):
            zl_copy(n, m4(zh - k)).wait_send()
    for n in range(4):
        zc_copy(m4(zl - (0, 1, -1, 2)[n]), n).wait_send()

    def main_rows(ref, core, cols=slice(None)):
        return ref[core, :, 0:64, cols].reshape(MAIN, -1)

    def tail_rows(core, cols=slice(None)):
        return x80[core, :, 64:80, cols].reshape(TAIL, -1)

    first, second_half = pl.ds(MAIN, TAIL), pl.ds(MAIN + TAIL, TAIL)

    def project(i):
        cols = pl.ds(pl.multiple_of(i * 384, 128), 384)
        main = hidp[:, 0:MAIN]
        pr[0, :, cols] = (dot(main, main_rows(x80, 0, cols)) + dot(hidp[:, first], tail_rows(0, cols))).astype(BF)
        pr[1, :, cols] = (dot(main, main_rows(x64, 0, cols)) + dot(hidp[:, second_half], tail_rows(0, cols))).astype(BF)
        pr[2, :, cols] = (dot(main, main_rows(x64, 1, cols)) + dot(hidp[:, first], tail_rows(1, cols))).astype(BF)

    pl.loop(0, 3)(project)
    ga = dot(gated[...], main_rows(x80, 1), RHS_T).astype(BF)
    ga_tail = dot(gated[...], tail_rows(1), RHS_T).astype(BF)
    pr[3] = (dot(ga, table[:, 0:MAIN], RHS_T) + dot(ga_tail, table[:, second_half], RHS_T)).astype(BF)

    acc[...] = jnp.zeros_like(acc)
    score_scale = 1.0 / math.sqrt(HD)
    same = (iota((256, 256), 0) & 3) == (iota((256, 256), 1) & 3)

    def head(i):
        first = jnp.minimum((i * HD) // 128, 7)
        cols = pl.ds(pl.multiple_of(first * 128, 128), 256)
        lane = iota((256, 256), 1) - (i * HD - first * 128)
        inside = (lane >= 0) & (lane < HD)
        zero = jnp.zeros((256, 256), BF)
        query = jnp.where(inside, pr[0, :, cols], zero)
        keys = jnp.where(inside, pr[1, :, cols], zero)
        values = pr[2, :, cols]
        grad = jnp.where(inside, pr[3, :, cols], zero)
        scores = dot(keys, query, RHS_T) * score_scale
        e = jnp.exp(jnp.where(same, scores, -jnp.inf))
        probs = e * (1.0 / jnp.sum(e, axis=0, keepdims=True))
        grad_probs = dot(values, grad, RHS_T)
        inner = jnp.sum(probs * grad_probs, axis=0, keepdims=True)
        grad_scores = (probs * (grad_probs - inner) * score_scale).astype(BF)
        acc[0, :, cols] += dot(grad_scores, keys, LHS_T)
        acc[1, :, cols] += dot(grad_scores, query)
        acc[2, :, cols] += dot(probs.astype(BF), grad)

    pl.loop(0, H)(head)
    for k in range(3):
        gp[k] = acc[k].astype(BF)

    gq, gk, gv = gp[0], gp[1], gp[2]
    back_main = (
        dot(gq, main_rows(x80, 0), RHS_T) + dot(gk, main_rows(x64, 0), RHS_T) + dot(gv, main_rows(x64, 1), RHS_T)
    )
    back_first = dot(gq, tail_rows(0), RHS_T) + dot(gv, tail_rows(1), RHS_T)
    back_second = dot(gk, tail_rows(0), RHS_T)
    for part, lanes in ((back_main, pl.ds(0, MAIN)), (back_first, first), (back_second, second_half)):
        top = part.astype(BF)
        hidp[:, lanes] = top
        gh_low[:, lanes] = (part - top.astype(F32)).astype(BF)
    acc[2] = dot(hidp[...], table[...], RHS_T) + dot(gh_low[...], table[...], RHS_T)

    sums[...] = jnp.zeros_like(sums)

    def norm_back(i):
        rows = pl.ds(pl.multiple_of(i * 32, 32), 32)
        inside = pl.ds(pl.multiple_of(lax.rem(i, 2) * 32, 32), 32)
        gh = acc[2, rows, :]
        nrm = normed[rows, :]
        second = clip_of((32, D))
        zero = jnp.zeros_like(gh)
        cross = gh * nrm
        sums[0:1, :] += jnp.sum(jnp.where(second, zero, gh), axis=0, keepdims=True)
        sums[1:2, :] += jnp.sum(jnp.where(second, zero, cross), axis=0, keepdims=True)
        sums[2:3, :] += jnp.sum(jnp.where(second, gh, zero), axis=0, keepdims=True)
        sums[3:4, :] += jnp.sum(jnp.where(second, cross, zero), axis=0, keepdims=True)
        gn = gh * (1.0 + jnp.where(second, mod_ref[1, 1:2, :], mod_ref[1, 0:1, :]))
        mean_grad = jnp.sum(gn, axis=1, keepdims=True) * (1.0 / D)
        mean_cross = jnp.sum(gn * nrm, axis=1, keepdims=True) * (1.0 / D)
        cot = rb.at[1, i // 2][inside, :].astype(F32)
        gt = cot + inv[rows, 0:1] * (gn - mean_grad - nrm * mean_cross)
        rr.at[0, i // 2][inside, :] = gt.astype(BF)

    pl.loop(0, 8)(norm_back)

    ms[0, 0:4, :] = sums[0:4, 0:640]
    ms[0, 4:8, 0:512] = sums[0:4, 640:1152]
    ms[0, 4:8, 512:640] = jnp.zeros((4, 128), F32)
    places = (zl, x, y)

    def m_copy(step, k):
        to = (at_zl(k), dev(m4(x + k), y, zfull, c), dev(x, m4(y + k), zfull, c))[step]
        return copy(ms.at[step], mr.at[step, places[step]], m_s.at[step, k], m_r.at[step, k], to)

    def m_start(step):
        for k in (1, 2, 3):
            m_copy(step, k).start()
        mr[step, places[step]] = ms[step]

    def m_sum(step):
        for k in (1, 2, 3):
            m_copy(step, k).wait()
        return ((mr[step, 0] + mr[step, 1]) + mr[step, 2]) + mr[step, 3]

    m_start(0)
    pieces = (pl.ds(0, 640), pl.ds(640, 512))

    def back_copy(n, k):
        return copy(rr.at[0, m4(zl + k), :, pieces[n]], rr.at[1, zl, :, pieces[n]], c_s.at[n, k], c_r.at[n, k], at_zl(k))

    for n in range(2):
        for k in (2, 1, 3):
            back_copy(n, k).start()
    rr[1, zl] = rr[0, zl]
    ms[1] = m_sum(0)
    m_start(1)

    from_line = pick(lambda o: ((o >> 1) & 3) * 64 + (o >> 4) * 4 + ((o >> 3) & 1) * 2 + (o & 1))

    def e_copy(n, k):
        return copy(rr2.at[0, m4(x + k // 4) * 4 + m4(y + lax.rem(k, 4)), :, pieces[n]],
                    rr2.at[1, xy, :, pieces[n]], e_s.at[n, k], e_r.at[n, k], at_xy(k))

    for n in range(2):
        for k in (1, 2, 3):
            back_copy(n, k).wait()
        lanes = pieces[n]
        rr2[0, :, :, lanes] = dot(from_line, rr[1, :, :, lanes].reshape(256, -1)).astype(BF).reshape(16, 16, -1)

        @pl.loop(1, 16)
        def _(k, n=n):
            e_copy(n, k).start()

        if n == 0:
            ms[2] = m_sum(1)
            m_start(2)

    rr2[1, xy] = rr2[0, xy]
    outm_ref[...] = m_sum(2)
    for n in range(2):
        @pl.loop(1, 16)
        def _(k, n=n):
            e_copy(n, k).wait()

    store = pltpu.make_async_copy(rr2.at[1], out_hbm, out_sem)
    store.start()
    store.wait()


def local(tokens, modulation, cotangent, qkv_weight, out_weight):
    table = jnp.asarray(place_table(), BF)
    hbm = pl.BlockSpec(memory_space=pl.ANY)
    dma = pltpu.SemaphoreType.DMA
    vmem = pltpu.VMEM
    rows, sums = pl.pallas_call(
        kernel,
        out_shape=(
            jax.ShapeDtypeStruct((16, 16, D), BF),
            jax.ShapeDtypeStruct((8, 640), F32),
        ),
        in_specs=[hbm] * 6,
        out_specs=(hbm, pl.BlockSpec(memory_space=pltpu.VMEM)),
        scratch_shapes=[
            vmem((2, 2, 128, D), BF),
            vmem((3, 2, D), F32),
            vmem((18, 432), BF),
            vmem((18, 144), BF),
            vmem((2, 16, 16, D), BF),
            vmem((2, 16, 16, D), BF),
            vmem((2, 4, 64, D), BF),
            vmem((2, 4, 64, D), BF),
            vmem((2, 4, 4, 16, 768), BF),
            vmem((2, 16, 80, D), BF),
            vmem((2, 16, 64, D), BF),
            vmem((D, MAIN + 2 * TAIL), BF),
            vmem((256, D), BF),
            vmem((256, MAIN + 2 * TAIL), BF),
            vmem((256, D), BF),
            vmem((256, D), F32),
            vmem((256, 128), F32),
            vmem((4, 256, D), BF),
            vmem((3, 256, D), F32),
            vmem((3, 256, D), BF),
            vmem((256, MAIN + 2 * TAIL), BF),
            vmem((2, 4, 64, D), BF),
            vmem((2, 16, 16, D), BF),
            vmem((8, D), F32),
            vmem((3, 8, 640), F32),
            vmem((3, 4, 8, 640), F32),
            dma((6,)), dma,
            dma((4,)), dma((4,)), dma((3, 4)), dma((3, 4)), dma((4,)), dma((4,)),
            dma((2, 16)), dma((2, 16)), dma((2, 16)), dma((2, 16)),
            dma((2, 16)), dma((2, 16)), dma((2, 4)), dma((2, 4)),
            dma((2, 4)), dma((2, 4)), dma((2, 16)), dma((2, 16)),
            dma((3, 4)), dma((3, 4)),
        ],
        compiler_params=pltpu.CompilerParams(
            collective_id=0, has_side_effects=True, vmem_limit_bytes=60 * 1024 * 1024
        ),
        name="sublayer_backward",
    )(
        tokens.reshape(2, 128, D), modulation.transpose(1, 0, 2), cotangent.reshape(2, 128, D),
        qkv_weight, out_weight, table,
    )
    grad_tokens = rows.reshape(16, 2, 8, D).transpose(1, 0, 2, 3).reshape(2, 1, 128, D)
    grad_modulation = jnp.concatenate([sums[0:4, :], sums[4:8, :512]], axis=1).reshape(2, 2, D)
    return grad_tokens, grad_modulation


def solution(mesh):
    in_specs = (
        P("dp", "seq", None, None),
        P("dp", None, None),
        P("dp", "seq", None, None),
        P("seq", "dp"),
        P("seq", "dp"),
    )
    out_specs = (P("dp", "seq", None, None), P("dp", None, None))
    return jax.shard_map(local, mesh=mesh, in_specs=in_specs, out_specs=out_specs, check_vma=False)
```

```python
import functools
import math

import jax
import jax.numpy as jnp
import numpy as np
from jax import lax
from jax.experimental import pallas as pl
from jax.experimental.pallas import tpu as pltpu
from jax.sharding import PartitionSpec as P

D = 1152
H = 16
PAIRS_AT_ONCE = 8
HD = 72
EPS = 1e-06
MESH = pl.DeviceIdType.MESH
BF = jnp.bfloat16
F32 = jnp.float32
RHS_T = (((1,), (1,)), ((), ()))
LHS_T = (((0,), (0,)), ((), ()))


MAIN, TAIL = 1024, 256


def place_table():
    table = np.zeros((MAIN + 2 * TAIL, D), np.float32)
    for feature in range(D):
        zl, rest = divmod(feature, 288)
        position, i = divmod(rest, 18)
        t = zl * 18 + i
        if t < 64:
            table[position * 64 + t, feature] = 1
        else:
            table[MAIN + position * 16 + t - 64, feature] = 1
            table[MAIN + TAIL + position * 16 + 8 + t - 64, feature] = 1
    return table


def dot(a, b, dims=(((1,), (0,)), ((), ()))):
    return lax.dot_general(a, b, dims, preferred_element_type=F32)


def iota(shape, dim):
    return lax.broadcasted_iota(jnp.int32, shape, dim)


def pick(source_row, n=256, m=256):
    return (source_row(iota((n, m), 0)) == iota((n, m), 1)).astype(F32).astype(BF)


def kernel(
    tok_hbm, mod_hbm, cot_hbm, wq_hbm, wo_hbm, table_hbm,
    out_hbm, outm_ref,
    raw, mod_ref, wq_ref, wo_ref,
    sa, ra, sb, rb, z, x80, x64, table, hid, hidg, hidt, gated, normed, inv, acc, pr, heads_acc, gp, gh_rows, gh, rr, rr2, out, ms, mr,
    in_sem, out_sem, zh_s, zh_r, zl_s, zl_r, zc_s, zc_r, w_s, w_r, wc_s, wc_r,
    a_s, a_r, b_s, b_r, c_s, c_r, e_s, e_r, m_s, m_r,
):
    s, q = lax.axis_index("seq"), lax.axis_index("dp")
    y, x, zl = lax.rem(s, 4), lax.rem(s // 4, 4), s // 16
    zh, c = q // 2, lax.rem(q, 2)
    xy = x * 4 + y
    zfull = zh * 4 + zl

    def m4(v):
        return lax.rem(v + 8, 4)

    def dev(x_, y_, z_, c_):
        return ((lax.rem(z_, 4) * 4 + x_) * 4 + y_, (z_ // 4) * 2 + c_)

    def at_xy(k):
        return dev(m4(x + k // 4), m4(y + lax.rem(k, 4)), zfull, c)

    def at_zl(k):
        return dev(x, y, zh * 4 + m4(zl + k), c)

    def at_zh(k):
        return dev(x, y, m4(zh + k) * 4 + zl, c)

    def at_ring(k):
        return dev(x, y, lax.rem(zfull + k + 16, 16), c)

    other = dev(x, y, zfull, 1 - c)

    def copy(src, dst, ss, rs, to):
        return pltpu.make_async_remote_copy(
            src_ref=src, dst_ref=dst, send_sem=ss, recv_sem=rs, device_id=to, device_id_type=MESH
        )

    loads = [
        pltpu.make_async_copy(src, dst, in_sem.at[n])
        for n, (src, dst) in enumerate((
            (wq_hbm, wq_ref), (wo_hbm, wo_ref), (tok_hbm, raw.at[0]), (cot_hbm, raw.at[1]),
            (mod_hbm, mod_ref), (table_hbm, table),
        ))
    ]
    for load in loads:
        load.start()

    barrier = pltpu.get_barrier_semaphore()

    def greet(to):
        pl.semaphore_signal(barrier, inc=1, device_id=to, device_id_type=MESH)

    for k in (1, 2, 3):
        greet(at_zh(k))
        greet(at_zl(k))
    for k in (1, -1, 2, -2):
        greet(at_ring(k))
    greet(other)

    @pl.loop(1, 16)
    def _(k):
        greet(at_xy(k))

    loads[0].wait()
    loads[1].wait()
    wide = jnp.concatenate(
        [wq_ref[...].astype(F32), wo_ref[...].astype(F32), jnp.zeros((18, 64), F32)], axis=1
    )
    ends = [wide[16 + j:17 + j, 128 * m:128 * m + 128] for j in range(2) for m in range(5)]
    ends = jnp.concatenate(ends + [jnp.zeros((6, 128), F32)], axis=0)
    z[c, zl, zh] = jnp.concatenate([wide[:16], ends], axis=1).astype(BF)

    to_plane = pick(lambda o: ((o >> 3) & 1) * 128 + (o >> 4) * 8 + (o & 7))

    def first_order(n):
        loads[2 + n].wait()
        sa[n] = dot(to_plane, raw[n].reshape(256, D)).astype(BF).reshape(16, 16, D)

    first_order(0)
    pl.semaphore_wait(barrier, 26)

    def zh_copy(k):
        ref = z.at[c, zl, zh]
        return copy(ref, ref, zh_s.at[k], zh_r.at[k], at_zh(k))

    ring = (1, -1, 2)

    def zl_copy(n, group):
        ref = z.at[c, zl, group]
        return copy(ref, ref, zl_s.at[n, group], zl_r.at[n, group], at_ring(ring[n]))

    def zl_arrived(n, group):
        ref = z.at[c, m4(zl - ring[n]), group]
        copy(ref, ref, zl_s.at[n, group], zl_r.at[n, group], at_ring(ring[n])).wait_recv()

    def zc_copy(line, n):
        ref = z.at[c, line]
        return copy(ref, ref, zc_s.at[n], zc_r.at[n], other)

    for k in (2, 1, 3):
        zh_copy(k).start()
    for n in range(3):
        zl_copy(n, zh).start()

    def a_copy(n, k):
        return copy(sa.at[n, m4(x + k // 4) * 4 + m4(y + lax.rem(k, 4))], ra.at[n, xy],
                    a_s.at[n, k], a_r.at[n, k], at_xy(k))

    def a_send(n):
        @pl.loop(1, 16)
        def _(k):
            a_copy(n, k).start()

        ra[n, xy] = sa[n, xy]

    a_send(0)
    first_order(1)
    a_send(1)

    for k in (1, 3, 2):
        zh_copy(k).wait_recv()
        for n in range(3):
            zl_copy(n, m4(zh - k)).start()
    zc_copy(zl, 0).start()

    def b_copy(n, k):
        return copy(sb.at[n, m4(zl + k)], rb.at[n, zl], b_s.at[n, k], b_r.at[n, k], at_zl(k))

    to_line = pick(lambda o: ((o >> 1) & 15) * 16 + ((o >> 5) & 1) * 8 + (o >> 6) * 2 + (o & 1))

    def second_step(n):
        @pl.loop(1, 16)
        def _(k):
            a_copy(n, k).wait()

        sb[n] = dot(to_line, ra[n].reshape(256, D)).astype(BF).reshape(4, 64, D)
        for k in (2, 1, 3):
            b_copy(n, k).start()
        rb[n, zl] = sb[n, zl]

    second_step(0)
    for n in range(3):
        for k in range(4):
            zl_arrived(n, m4(zh - k))
        zc_copy(m4(zl - ring[n]), 1 + n).start()
    for n in range(4):
        ref = z.at[1 - c, m4(zl - (0, 1, -1, 2)[n])]
        copy(ref, ref, zc_s.at[n], zc_r.at[n], other).wait_recv()

    def block(d):
        parts = []
        for k in range(4):
            stored = z[d % 2, k, d // 2].astype(F32)
            parts.append(stored[:, :640])
            for j in range(2):
                parts.append(jnp.concatenate(
                    [stored[5 * j + m:5 * j + m + 1, 640:768] for m in range(5)], axis=1
                ))
        return jnp.concatenate(parts, axis=0)

    blocks = [block(d) for d in range(8)]
    full = jnp.concatenate([b[:, :432] for b in blocks] + [b[:, 432:576] for b in blocks], axis=1)
    quarters = [full[:, k * D:(k + 1) * D] for k in range(4)]
    x80[0, x, y, 0:64, :] = quarters[0][:64].astype(BF)
    x80[0, x, y, 64:80, :] = jnp.concatenate([quarters[0][64:], quarters[1][64:]], axis=0).astype(BF)
    x64[0, x, y] = quarters[1][:64].astype(BF)
    x80[1, x, y, 0:64, :] = quarters[3][:64].astype(BF)
    x80[1, x, y, 64:80, :] = jnp.concatenate([quarters[2][64:], quarters[3][64:]], axis=0).astype(BF)
    x64[1, x, y] = quarters[2][:64].astype(BF)

    stores = (x80, x64)
    first_axis = (((1 - c), c), (c, (1 - c)))

    def shifted(st, i, j):
        fx, fy = first_axis[st]
        return m4(x + i * fx + j * fy), m4(y + i * fy + j * fx)

    def held(st, i, j):
        px, py = shifted(st, i, j)
        return stores[st].at[c, px, py]

    sent = []

    def w_send(st, i, j, to_i, to_j):
        ref = held(st, i, j)
        px, py = shifted(st, to_i, to_j)
        index = ((i - to_i) % 4) * 4 + (j - to_j) % 4
        cp = copy(ref, ref, w_s.at[st, index], w_r.at[st, index], dev(px, py, zfull, c))
        cp.start()
        sent.append(cp)

    def w_arrived(st, i, j):
        ref = held(st, i, j)
        index = i * 4 + j
        copy(ref, ref, w_s.at[st, index], w_r.at[st, index], other).wait_recv()
        cp = copy(ref, ref, wc_s.at[st, index], wc_r.at[st, index], other)
        cp.start()
        sent.append(cp)

    def w_both_ways(st, i):
        w_send(st, i, 0, 0, 1)
        w_send(st, i, 0, 0, -1)

    def w_sides(st, i):
        w_arrived(st, i, 3)
        if i in (0, 2):
            w_send(st, i, 3, 0, 1)
        w_arrived(st, i, 1)
        if i in (1, 3):
            w_send(st, i, 1, 0, -1)

    for st in range(2):
        for i in (1, -1, 2):
            w_send(st, 0, 0, i, 0)
        w_both_ways(st, 0)

    second_step(1)
    for i in (1, 3):
        for st in range(2):
            w_arrived(st, i, 0)
            w_both_ways(st, i)
    for st in range(2):
        w_sides(st, 0)
    for st in range(2):
        w_arrived(st, 2, 0)
        w_both_ways(st, 2)

    def places_of(i):
        clip, line = lax.rem(i, 2), i // 2
        rows = pl.ds(pl.multiple_of(clip * 128 + line * 32, 32), 32)
        return clip, line, rows, pl.ds(pl.multiple_of(clip * 32, 32), 32)

    def norm_rows(i):
        clip, line, rows, source = places_of(i)
        tile = rb.at[0, line][source, :].astype(F32)
        mean = jnp.sum(tile, axis=1, keepdims=True) * (1.0 / D)
        centred = tile - mean
        inv_std = lax.rsqrt(jnp.sum(centred * centred, axis=1, keepdims=True) * (1.0 / D) + EPS)
        nrm = centred * inv_std
        normed[rows, :] = nrm
        inv[rows, :] = jnp.broadcast_to(inv_std, (32, 128))
        hid[rows, :] = (nrm * (1.0 + mod_ref[1, pl.ds(clip, 1), :]) + mod_ref[0, pl.ds(clip, 1), :]).astype(BF)

    def gate_rows(i):
        clip, line, rows, source = places_of(i)
        cot = rb.at[1, line][source, :].astype(F32)
        gated[rows, :] = (cot * mod_ref[2, pl.ds(clip, 1), :]).astype(BF)

    def hidden_in(places):
        return dot(hid[...], places, RHS_T).astype(BF)

    def table_column(yj):
        return jnp.concatenate(
            [table[pl.ds(pl.multiple_of((k * 4 + yj) * 64, 64), 64), :] for k in range(4)], axis=0
        )

    def table_row(xj):
        return table[pl.ds(pl.multiple_of(xj * 256, 256), 256), :]

    def project(j, last=False):
        xj, yj = m4(x + j), m4(y + j)

        def columns(i):
            cols = pl.ds(pl.multiple_of(i * 384, 128), 384)
            sums_now = [
                dot(hidg[j, 0], x80[0, :, yj, 0:64, cols].reshape(256, 384)),
                dot(hidg[j, 1], x64[0, xj, :, :, cols].reshape(256, 384)),
                dot(hidg[j, 0], x64[1, :, yj, :, cols].reshape(256, 384)),
            ]
            for k in range(3):
                if j == 0:
                    acc[k, :, cols] = sums_now[k]
                elif not last:
                    acc[k, :, cols] += sums_now[k]
                else:
                    tail = x80[k // 2, :, :, 64:80, cols].reshape(TAIL, 384)
                    pr[k, :, cols] = (acc[k, :, cols] + sums_now[k] + dot(hidt[k % 2], tail)).astype(BF)

        pl.loop(0, 3)(columns)

    def project_grad(j, last=False):
        xj = m4(x + j)
        ga = dot(gated[...], x80[1, xj, :, 0:64, :].reshape(256, D), RHS_T).astype(BF)
        now = dot(ga, table_row(xj))
        if j == 0:
            acc[3] = now
        elif not last:
            acc[3] += now
        else:
            ga = dot(gated[...], x80[1, :, :, 64:80, :].reshape(TAIL, D), RHS_T).astype(BF)
            pr[3] = (acc[3] + now + dot(ga, table[MAIN + TAIL:MAIN + 2 * TAIL, :])).astype(BF)

    def w_across(i, j):
        for st in range(2):
            px, py = shifted(1 - st, i, j)
            ref = stores[st].at[1 - c, px, py]
            index = i * 4 + j
            copy(ref, ref, wc_s.at[st, index], wc_r.at[st, index], other).wait_recv()

    for k in (1, 2, 3):
        b_copy(0, k).wait()
    for load in loads[4:]:
        load.wait()
    pl.loop(0, 8)(norm_rows)
    for k in range(2):
        hidt[k] = hidden_in(table[MAIN + k * TAIL:MAIN + (k + 1) * TAIL, :])
    for j in range(4):
        hidg[j, 0] = hidden_in(table_column(m4(y + j)))
        hidg[j, 1] = hidden_in(table_row(m4(x + j)))
    for st in range(2):
        w_sides(st, 1)
    for i in (1, 2, 3):
        w_across(i, 0)
    project(0)
    for i in (3, 2):
        for st in range(2):
            w_sides(st, i)
    for j in (3, 1):
        for i in range(4):
            w_across(i, j)
        project(j)
    for k in (1, 2, 3):
        b_copy(1, k).wait()
    pl.loop(0, 8)(gate_rows)
    for j in (0, 3, 1):
        project_grad(j)
    for i in range(4):
        for st in range(2):
            w_arrived(st, i, 2)
    for i in range(4):
        w_across(i, 2)
    project(2, last=True)
    project_grad(2, last=True)
    for cp in sent:
        cp.wait_send()
    for k in (1, 2, 3):
        zh_copy(k).wait_send()
    for n in range(3):
        for k in range(4):
            zl_copy(n, m4(zh - k)).wait_send()
    for n in range(4):
        zc_copy(m4(zl - (0, 1, -1, 2)[n]), n).wait_send()

    def main_rows(ref, core):
        return ref[core, :, :, 0:64, :].reshape(MAIN, D)

    def tail_rows(core):
        return x80[core, :, :, 64:80, :].reshape(TAIL, D)

    score_scale = 1.0 / math.sqrt(HD)
    same = (iota((128, 256), 0) & 1) == (iota((128, 256), 1) & 1)

    def attend(clip):
        rows = pl.ds(clip * 128, 128)
        heads_acc[...] = jnp.zeros_like(heads_acc)

        def head_pair(i):
            first = (i * 2 * HD) // 128
            cols = pl.ds(pl.multiple_of(first * 128, 128), 256)
            lane = iota((128, 256), 1) - (i * 2 * HD - first * 128)
            zero = jnp.zeros((128, 256), BF)

            def by_head(window):
                return jnp.concatenate([
                    jnp.where((lane >= 0) & (lane < HD), window, zero),
                    jnp.where((lane >= HD) & (lane < 2 * HD), window, zero),
                ], axis=0)

            keys, values = pr[1, rows, cols], pr[2, rows, cols]
            queries, grads = by_head(pr[0, rows, cols]), by_head(pr[3, rows, cols])
            scores = dot(keys, queries, RHS_T) * score_scale
            e = jnp.exp(jnp.where(same, scores, -jnp.inf))
            probs = e * (1.0 / jnp.sum(e, axis=0, keepdims=True))
            grad_probs = dot(values, grads, RHS_T)
            inner = jnp.sum(probs * grad_probs, axis=0, keepdims=True)
            grad_scores = (probs * (grad_probs - inner) * score_scale).astype(BF)
            upright = jnp.concatenate([grad_scores[:, 0:128], grad_scores[:, 128:256]], axis=0)
            heads_acc[0, :, cols] += dot(upright, by_head(keys), LHS_T)
            heads_acc[1, :, cols] += dot(grad_scores, queries)
            heads_acc[2, :, cols] += dot(probs.astype(BF), grads)

        pl.loop(0, H // 2, unroll=PAIRS_AT_ONCE)(head_pair)
        for k in range(3):
            gp[k] = heads_acc[k].astype(BF)

    def back_rows(clip):
        gq, gk, gv = gp[0], gp[1], gp[2]
        gh_rows[:, 0:MAIN] = (
            dot(gq, main_rows(x80, 0), RHS_T) + dot(gk, main_rows(x64, 0), RHS_T) + dot(gv, main_rows(x64, 1), RHS_T)
        ).astype(BF)
        tails = dot(gp[0:2].reshape(256, D), tail_rows(0), RHS_T)
        gh_rows[:, MAIN:MAIN + TAIL] = (tails[0:128] + dot(gv, tail_rows(1), RHS_T)).astype(BF)
        gh_rows[:, MAIN + TAIL:MAIN + 2 * TAIL] = tails[128:256].astype(BF)
        gh[...] = dot(gh_rows[...], table[...])

        shift_sum = jnp.sum(gh[...], axis=0, keepdims=True)
        scale_sum = jnp.sum(gh[...] * normed[clip * 128:clip * 128 + 128, :], axis=0, keepdims=True)
        for n, row in enumerate((shift_sum, scale_sum)):
            n += 2 * clip
            ms[0, n:n + 1, :] = row[:, 0:640]
            ms[0, n + 4:n + 5, 0:512] = row[:, 640:1152]
            ms[0, n + 4:n + 5, 512:640] = jnp.zeros((1, 128), F32)
        if clip == 1:
            m_start(0)

        def norm_back(line):
            rows = pl.ds(pl.multiple_of(clip * 128 + line * 32, 32), 32)
            grad_hidden = gh[pl.ds(pl.multiple_of(line * 32, 32), 32), :]
            nrm = normed[rows, :]
            gn = grad_hidden * (1.0 + mod_ref[1, clip:clip + 1, :])
            mean_grad = jnp.sum(gn, axis=1, keepdims=True) * (1.0 / D)
            mean_cross = jnp.sum(gn * nrm, axis=1, keepdims=True) * (1.0 / D)
            cot = rb.at[1, line][clip * 32:clip * 32 + 32, :].astype(F32)
            gt = cot + inv[rows, 0:1] * (gn - mean_grad - nrm * mean_cross)
            rr.at[0, line][clip * 32:clip * 32 + 32, :] = gt.astype(BF)

        for k in (2, 1, 3):
            norm_back(m4(zl + k))
            back_copy(clip, k).start()
        norm_back(zl)
        rr.at[1, zl][clip * 32:clip * 32 + 32, :] = rr.at[0, zl][clip * 32:clip * 32 + 32, :]

    def back_copy(clip, k):
        part = pl.ds(clip * 32, 32)
        return copy(rr.at[0, m4(zl + k), part], rr.at[1, zl, part], c_s.at[clip, k], c_r.at[clip, k], at_zl(k))

    def e_copy(clip, k):
        return copy(rr2.at[0, clip, m4(x + k // 4) * 4 + m4(y + k % 4)], rr2.at[1, clip, xy],
                    e_s.at[clip, k], e_r.at[clip, k], at_xy(k))

    def line_row(o):
        return ((o >> 1) & 3) * 32 + (o >> 4) * 2 + (o & 1)

    both_halves = pick(lambda o: line_row(o) + ((o >> 3) & 1) * 128)
    top_half = pick(lambda o: jnp.where(((o >> 3) & 1) == 0, line_row(o), -1), 256, 128)

    def plane_start(clip):
        for k in (1, 2, 3):
            back_copy(clip, k).wait()
        block = rr[1, :, clip * 32:clip * 32 + 32, :].reshape(128, D)
        stacked = jnp.concatenate([block[:, 0:512], block[:, 640:1152]], axis=0)
        rr2[0, clip, :, :, 0:512] = dot(both_halves, stacked).astype(BF).reshape(16, 16, 512)
        rr2[0, clip, :, :, 512:640] = dot(top_half, block[:, 512:640]).astype(BF).reshape(16, 16, 128)

        for k in range(1, 16):
            e_copy(clip, k).start()

        rr2[1, clip, xy] = rr2[0, clip, xy]

    upper = pick(lambda o: (o >> 3) * 16 + (o & 7), 128, 256)
    lower = pick(lambda o: (o >> 3) * 16 + 8 + (o & 7), 128, 256)

    def finish(clip):
        for k in range(1, 16):
            e_copy(clip, k).wait()

        rows = rr2[1, clip].reshape(256, 640)
        out[clip, :, 0:640] = dot(upper, rows).astype(BF)
        out[clip, :, 640:1152] = dot(lower, rows[:, 0:512]).astype(BF)
        cp = pltpu.make_async_copy(out.at[clip], out_hbm.at[clip], out_sem.at[clip])
        cp.start()
        return cp

    places = (zl, x, y)

    def m_copy(step, k):
        to = (at_zl(k), dev(m4(x + k), y, zfull, c), dev(x, m4(y + k), zfull, c))[step]
        return copy(ms.at[step], mr.at[step, places[step]], m_s.at[step, k], m_r.at[step, k], to)

    def m_start(step):
        for k in (1, 2, 3):
            m_copy(step, k).start()
        mr[step, places[step]] = ms[step]

    def m_sum(step):
        for k in (1, 2, 3):
            m_copy(step, k).wait()
        return ((mr[step, 0] + mr[step, 1]) + mr[step, 2]) + mr[step, 3]

    attend(0)
    back_rows(0)
    attend(1)
    plane_start(0)
    back_rows(1)
    ms[1] = m_sum(0)
    m_start(1)
    stored_first = finish(0)
    ms[2] = m_sum(1)
    m_start(2)
    plane_start(1)
    total = m_sum(2)
    for clip in range(2):
        outm_ref[clip, :, 0:640] = total[2 * clip:2 * clip + 2]
        outm_ref[clip, :, 640:1152] = total[4 + 2 * clip:6 + 2 * clip, 0:512]
    stored_second = finish(1)
    stored_first.wait()
    stored_second.wait()


def local(tokens, modulation, cotangent, qkv_weight, out_weight):
    table = jnp.asarray(place_table(), BF)
    hbm = pl.BlockSpec(memory_space=pl.ANY)
    dma = pltpu.SemaphoreType.DMA
    vmem = pltpu.VMEM
    grad_tokens, grad_modulation = pl.pallas_call(
        kernel,
        out_shape=(
            jax.ShapeDtypeStruct((2, 128, D), BF),
            jax.ShapeDtypeStruct((2, 2, D), F32),
        ),
        in_specs=[hbm] * 6,
        out_specs=(hbm, pl.BlockSpec(memory_space=pltpu.VMEM)),
        scratch_shapes=[
            vmem((2, 2, 128, D), BF),
            vmem((3, 2, D), F32),
            vmem((18, 432), BF),
            vmem((18, 144), BF),
            vmem((2, 16, 16, D), BF),
            vmem((2, 16, 16, D), BF),
            vmem((2, 4, 64, D), BF),
            vmem((2, 4, 64, D), BF),
            vmem((2, 4, 4, 16, 768), BF),
            vmem((2, 4, 4, 80, D), BF),
            vmem((2, 4, 4, 64, D), BF),
            vmem((MAIN + 2 * TAIL, D), BF),
            vmem((256, D), BF),
            vmem((4, 2, 256, 256), BF),
            vmem((2, 256, TAIL), BF),
            vmem((256, D), BF),
            vmem((256, D), F32),
            vmem((256, 128), F32),
            vmem((4, 256, D), F32),
            vmem((4, 256, D), BF),
            vmem((3, 128, D), F32),
            vmem((3, 128, D), BF),
            vmem((128, MAIN + 2 * TAIL), BF),
            vmem((128, D), F32),
            vmem((2, 4, 64, D), BF),
            vmem((2, 2, 16, 16, 640), BF),
            vmem((2, 128, D), BF),
            vmem((3, 8, 640), F32),
            vmem((3, 4, 8, 640), F32),
            dma((6,)), dma((2,)),
            dma((4,)), dma((4,)), dma((3, 4)), dma((3, 4)), dma((4,)), dma((4,)),
            dma((2, 16)), dma((2, 16)), dma((2, 16)), dma((2, 16)),
            dma((2, 16)), dma((2, 16)), dma((2, 4)), dma((2, 4)),
            dma((2, 4)), dma((2, 4)), dma((2, 16)), dma((2, 16)),
            dma((3, 4)), dma((3, 4)),
        ],
        compiler_params=pltpu.CompilerParams(
            collective_id=0, has_side_effects=True, vmem_limit_bytes=60 * 1024 * 1024
        ),
        name="sublayer_backward",
    )(
        tokens.reshape(2, 128, D), modulation.transpose(1, 0, 2), cotangent.reshape(2, 128, D),
        qkv_weight, out_weight, table,
    )
    return grad_tokens.reshape(2, 1, 128, D), grad_modulation


def solution(mesh):
    in_specs = (
        P("dp", "seq", None, None),
        P("dp", None, None),
        P("dp", "seq", None, None),
        P("seq", "dp"),
        P("seq", "dp"),
    )
    out_specs = (P("dp", "seq", None, None), P("dp", None, None))
    return jax.shard_map(local, mesh=mesh, in_specs=in_specs, out_specs=out_specs, check_vma=False)
```

```python
import functools
import math

import jax
import jax.numpy as jnp
import numpy as np
from jax import lax
from jax.experimental import pallas as pl
from jax.experimental.pallas import tpu as pltpu
from jax.sharding import PartitionSpec as P

D = 1152
H = 16
HD = 72
EPS = 1e-06
MESH = pl.DeviceIdType.MESH
BF = jnp.bfloat16
F32 = jnp.float32
RHS_T = (((1,), (1,)), ((), ()))
LHS_T = (((0,), (0,)), ((), ()))


MAIN, TAIL = 1024, 256


def place_table():
    table = np.zeros((MAIN + 2 * TAIL, D), np.float32)
    for feature in range(D):
        zl, rest = divmod(feature, 288)
        position, i = divmod(rest, 18)
        t = zl * 18 + i
        if t < 64:
            table[position * 64 + t, feature] = 1
        else:
            table[MAIN + position * 16 + t - 64, feature] = 1
            table[MAIN + TAIL + position * 16 + 8 + t - 64, feature] = 1
    return table


def dot(a, b, dims=(((1,), (0,)), ((), ()))):
    return lax.dot_general(a, b, dims, preferred_element_type=F32)


def iota(shape, dim):
    return lax.broadcasted_iota(jnp.int32, shape, dim)


def pick(source_row, n=256, m=256):
    return (source_row(iota((n, m), 0)) == iota((n, m), 1)).astype(F32).astype(BF)


def kernel(
    tok_hbm, mod_hbm, cot_hbm, wq_hbm, wo_hbm, table_hbm,
    out_hbm, outm_ref,
    raw, mod_ref, wq_ref, wo_ref,
    sa, ra, sb, rb, z, xs, xt, table, hid, hidg, hidt, gated, normed, inv, acc, acc_grad, pr, pr_grad, heads_acc, gp, gh_rows, gh, rr, rr2, out, ms, mr,
    in_sem, out_sem, zh_s, zh_r, zl_s, zl_r, w_s, w_r, wc_s, wc_r,
    a_s, a_r, b_s, b_r, c_s, c_r, e_s, e_r, m_s, m_r,
):
    s, q = lax.axis_index("seq"), lax.axis_index("dp")
    y, x, zl = lax.rem(s, 4), lax.rem(s // 4, 4), s // 16
    zh, c = q // 2, lax.rem(q, 2)
    xy = x * 4 + y
    zfull = zh * 4 + zl

    def m4(v):
        return lax.rem(v + 8, 4)

    def dev(x_, y_, z_, c_):
        return ((lax.rem(z_, 4) * 4 + x_) * 4 + y_, (z_ // 4) * 2 + c_)

    def at_xy(k):
        return dev(m4(x + k // 4), m4(y + lax.rem(k, 4)), zfull, c)

    def at_zl(k):
        return dev(x, y, zh * 4 + m4(zl + k), c)

    def at_zh(k):
        return dev(x, y, m4(zh + k) * 4 + zl, c)

    def at_ring(k):
        return dev(x, y, lax.rem(zfull + k + 16, 16), c)

    other = dev(x, y, zfull, 1 - c)

    def copy(src, dst, ss, rs, to):
        return pltpu.make_async_remote_copy(
            src_ref=src, dst_ref=dst, send_sem=ss, recv_sem=rs, device_id=to, device_id_type=MESH
        )

    loads = [
        pltpu.make_async_copy(src, dst, in_sem.at[n])
        for n, (src, dst) in enumerate((
            (wq_hbm, wq_ref), (wo_hbm, wo_ref), (tok_hbm, raw.at[0]), (cot_hbm, raw.at[1]),
            (mod_hbm, mod_ref), (table_hbm, table),
        ))
    ]
    for load in loads:
        load.start()

    barrier = pltpu.get_barrier_semaphore()

    def greet(to):
        pl.semaphore_signal(barrier, inc=1, device_id=to, device_id_type=MESH)

    for k in (1, 2, 3):
        greet(at_zh(k))
        greet(at_zl(k))
    for k in (1, -1, 2, -2):
        greet(at_ring(k))
    greet(other)

    @pl.loop(1, 16)
    def _(k):
        greet(at_xy(k))

    loads[0].wait()
    loads[1].wait()
    wide = jnp.concatenate(
        [wq_ref[...].astype(F32), wo_ref[...].astype(F32), jnp.zeros((18, 64), F32)], axis=1
    )
    ends = [wide[16 + j:17 + j, 128 * m:128 * m + 128] for j in range(2) for m in range(5)]
    ends = jnp.concatenate(ends + [jnp.zeros((6, 128), F32)], axis=0)
    z[zl, zh] = jnp.concatenate([wide[:16], ends], axis=1).astype(BF)

    to_plane = pick(lambda o: ((o >> 3) & 1) * 128 + (o >> 4) * 8 + (o & 7))

    def first_order(n):
        loads[2 + n].wait()
        sa[n] = dot(to_plane, raw[n].reshape(256, D)).astype(BF).reshape(16, 16, D)

    first_order(0)
    pl.semaphore_wait(barrier, 26)

    def zh_copy(k):
        ref = z.at[zl, zh]
        return copy(ref, ref, zh_s.at[k], zh_r.at[k], at_zh(k))

    ring = (1, -1, 2)

    def zl_copy(n, group):
        ref = z.at[zl, group]
        return copy(ref, ref, zl_s.at[n, group], zl_r.at[n, group], at_ring(ring[n]))

    def zl_arrived(n, group):
        ref = z.at[m4(zl - ring[n]), group]
        copy(ref, ref, zl_s.at[n, group], zl_r.at[n, group], at_ring(ring[n])).wait_recv()

    for k in (2, 1, 3):
        zh_copy(k).start()
    for n in range(3):
        zl_copy(n, zh).start()

    def a_copy(n, k):
        return copy(sa.at[n, m4(x + k // 4) * 4 + m4(y + lax.rem(k, 4))], ra.at[n, xy],
                    a_s.at[n, k], a_r.at[n, k], at_xy(k))

    def a_send(n):
        @pl.loop(1, 16)
        def _(k):
            a_copy(n, k).start()

        ra[n, xy] = sa[n, xy]

    a_send(0)
    first_order(1)
    a_send(1)

    for k in (1, 3, 2):
        zh_copy(k).wait_recv()
        for n in range(3):
            zl_copy(n, m4(zh - k)).start()

    def b_copy(n, k):
        return copy(sb.at[n, m4(zl + k)], rb.at[n, zl], b_s.at[n, k], b_r.at[n, k], at_zl(k))

    to_line = pick(lambda o: ((o >> 1) & 15) * 16 + ((o >> 5) & 1) * 8 + (o >> 6) * 2 + (o & 1))

    def second_step(n):
        @pl.loop(1, 16)
        def _(k):
            a_copy(n, k).wait()

        sb[n] = dot(to_line, ra[n].reshape(256, D)).astype(BF).reshape(4, 64, D)
        for k in (2, 1, 3):
            b_copy(n, k).start()
        rb[n, zl] = sb[n, zl]

    mine = zh // 2

    def rows_of(group):
        parts = []
        for k in range(4):
            stored = z[k, group].astype(F32)
            parts.append(stored[:, :640])
            for j in range(2):
                parts.append(jnp.concatenate(
                    [stored[5 * j + m:5 * j + m + 1, 640:768] for m in range(5)], axis=1
                ))
        return jnp.concatenate(parts, axis=0)

    def unit(half):
        for n in range(3):
            for b in range(2):
                zl_arrived(n, 2 * half + b)
        a, b = rows_of(2 * half), rows_of(2 * half + 1)
        return jnp.concatenate([a[:, :432], b[:, :432], a[:, 432:576], b[:, 432:576]], axis=1)

    first_axis = ((c, (1 - c)), ((1 - c), c))

    def shifted(st, i, j):
        fx, fy = first_axis[st]
        return m4(x + i * fx + j * fy), m4(y + i * fy + j * fx)

    def block_of(core, st, px, py):
        return xs.at[core, st, px, py, pl.ds(0, 64)] if st == 0 else xs.at[core, st, px, py]

    def held(st, i, j):
        px, py = shifted(st, i, j)
        return block_of(c, st, px, py)

    sent = []

    def w_send(st, i, j, to_i, to_j):
        ref = held(st, i, j)
        px, py = shifted(st, to_i, to_j)
        index = ((i - to_i) % 4) * 4 + (j - to_j) % 4
        cp = copy(ref, ref, w_s.at[st, index], w_r.at[st, index], dev(px, py, zfull, c))
        cp.start()
        sent.append(cp)

    def w_over(st, i, j):
        ref = held(st, i, j)
        index = i * 4 + j
        cp = copy(ref, ref, wc_s.at[st, index], wc_r.at[st, index], other)
        cp.start()
        sent.append(cp)

    def w_arrived(st, i, j):
        ref = held(st, i, j)
        index = i * 4 + j
        copy(ref, ref, w_s.at[st, index], w_r.at[st, index], other).wait_recv()
        w_over(st, i, j)

    def w_both_ways(st, i):
        w_send(st, i, 0, 0, 1)
        w_send(st, i, 0, 0, -1)

    def w_sides(st, i):
        w_arrived(st, i, 3)
        if i in (0, 2):
            w_send(st, i, 3, 0, 1)
        w_arrived(st, i, 1)
        if i in (1, 3):
            w_send(st, i, 1, 0, -1)

    def w_first(st):
        for i in (1, -1, 2):
            w_send(st, 0, 0, i, 0)
        w_both_ways(st, 0)
        w_over(st, 0, 0)

    second_step(0)
    near = unit(mine)
    xs[c, 0, x, y, 0:64, :] = near[:64].astype(BF)
    w_first(0)
    far = unit(1 - mine)
    xs[c, 1, x, y, 0:64, :] = far[:64].astype(BF)
    xs[c, 1, x, y, 64:80, :] = jnp.concatenate([
        jnp.where(mine == 0, near[64:], far[64:]), jnp.where(mine == 0, far[64:], near[64:])
    ], axis=0).astype(BF)
    w_first(1)
    second_step(1)
    for i in (1, 3):
        for st in range(2):
            w_arrived(st, i, 0)
            w_both_ways(st, i)
    for st in range(2):
        w_sides(st, 0)
    for st in range(2):
        w_arrived(st, 2, 0)
        w_both_ways(st, 2)

    def places_of(i):
        clip, lines = lax.rem(i, 2), pl.ds(pl.multiple_of(i // 2 * 2, 2), 2)
        rows = pl.ds(pl.multiple_of(clip * 128 + i // 2 * 64, 64), 64)
        return clip, lines, rows, pl.ds(pl.multiple_of(clip * 32, 32), 32)

    def norm_rows(i):
        clip, lines, rows, source = places_of(i)
        tile = rb[0, lines, source, :].reshape(64, D).astype(F32)
        mean = jnp.sum(tile, axis=1, keepdims=True) * (1.0 / D)
        centred = tile - mean
        inv_std = lax.rsqrt(jnp.sum(centred * centred, axis=1, keepdims=True) * (1.0 / D) + EPS)
        nrm = centred * inv_std
        normed[rows, :] = nrm
        inv[rows, :] = jnp.broadcast_to(inv_std, (64, 128))
        hid[rows, :] = (nrm * (1.0 + mod_ref[1, pl.ds(clip, 1), :]) + mod_ref[0, pl.ds(clip, 1), :]).astype(BF)

    def gate_rows(i):
        clip, lines, rows, source = places_of(i)
        cot = rb[1, lines, source, :].reshape(64, D).astype(F32)
        g = (cot * mod_ref[2, pl.ds(clip, 1), :]).astype(BF).astype(F32)
        for core in range(2):
            for half in range(2):
                d = 4 * half + core
                gated[core, half, rows, :] = jnp.concatenate([
                    jnp.zeros((64, 96), F32), g[:, 144 * d:144 * d + 144], g[:, 144 * d + 288:144 * d + 432]
                ], axis=1).astype(BF)

    def hidden_in(places):
        return dot(hid[...], places, RHS_T).astype(BF)

    def table_column(yj):
        return jnp.concatenate(
            [table[pl.ds(pl.multiple_of((k * 4 + yj) * 64, 64), 64), :] for k in range(4)], axis=0
        )

    def table_row(xj):
        return table[pl.ds(pl.multiple_of(xj * 256, 256), 256), :]

    def main_block(core, st, j, cols):
        if core != st:
            return xs[core, st, :, m4(y + j), 0:64, cols].reshape(256, -1)
        return xs[core, st, m4(x + j), :, 0:64, cols].reshape(256, -1)

    def tail_block(core, cols):
        return xs[core, 1, :, :, 64:80, cols].reshape(TAIL, -1)

    units = [(core, st) for core in range(2) for st in range(2)]

    def half_of(st):
        return lax.rem(mine + st, 2)

    def project(j, last=False):
        for core, st in units:
            for cols in (pl.ds(0, 512), pl.ds(512, 384)):
                now = dot(hidg[j, 0 if core != st else 1], main_block(core, st, j, cols))
                if j == 0:
                    acc[core, st, :, cols] = now
                elif not last:
                    acc[core, st, :, cols] += now
                else:
                    tail = dot(hidt[half_of(st)], tail_block(core, cols))
                    pr[core, half_of(st), :, cols] = (acc[core, st, :, cols] + now + tail).astype(BF)

    def by_columns_first(part):
        return jnp.concatenate([
            part[:, (b * 4 + a) * 64:(b * 4 + a) * 64 + 64] for a in range(4) for b in range(4)
        ], axis=1)

    def lanes_of(column, j):
        at = m4(y + j) if column else m4(x + j)
        return pl.ds(pl.multiple_of(at * 256, 256), 256)

    def upright_rows(j):
        for core, st in units:
            xt[core, st, :, lanes_of(core != st, j)] = main_block(core, st, j, pl.ds(0, 896)).T

    out_cols = pl.ds(768, 384)

    def project_grad(j):
        for column in (True, False):
            acc_grad[int(column), :, lanes_of(column, j)] = sum(
                dot(gated[core, half_of(st)], main_block(core, st, j, out_cols), RHS_T)
                for core, st in units if (core != st) == column
            )

    def place_grad():
        main = (acc_grad[0] + by_columns_first(acc_grad[1])).astype(BF)
        first, second = [
            sum(dot(gated[core, half], tail_block(core, out_cols), RHS_T) for core in range(2)) for half in range(2)
        ]
        ends = (first + pltpu.roll(second, TAIL - 8, 1)).astype(BF)
        pr_grad[...] = (dot(main, table[0:MAIN, :]) + dot(ends, table[MAIN:MAIN + TAIL, :])).astype(BF)

    def w_across(i, j):
        for st in range(2):
            px, py = shifted(1 - st, i, j)
            ref = block_of(1 - c, st, px, py)
            index = i * 4 + j
            copy(ref, ref, wc_s.at[st, index], wc_r.at[st, index], other).wait_recv()

    for k in (1, 2, 3):
        b_copy(0, k).wait()
    for load in loads[4:]:
        load.wait()
    pl.loop(0, 4)(norm_rows)
    for k in range(2):
        hidt[k] = hidden_in(table[MAIN + k * TAIL:MAIN + (k + 1) * TAIL, :])
    for j in range(4):
        hidg[j, 0] = hidden_in(table_column(m4(y + j)))
        hidg[j, 1] = hidden_in(table_row(m4(x + j)))
    for st in range(2):
        w_sides(st, 1)
    for i in range(4):
        w_across(i, 0)
    project(0)
    upright_rows(0)
    for i in (3, 2):
        for st in range(2):
            w_sides(st, i)
    for j in (3, 1):
        for i in range(4):
            w_across(i, j)
        project(j)
        upright_rows(j)
    for k in (1, 2, 3):
        b_copy(1, k).wait()
    pl.loop(0, 4)(gate_rows)
    for j in (0, 3, 1):
        project_grad(j)
    for i in range(4):
        for st in range(2):
            w_arrived(st, i, 2)
    for i in range(4):
        w_across(i, 2)
    project(2, last=True)
    project_grad(2)
    place_grad()
    upright_rows(2)
    for cp in sent:
        cp.wait_send()
    for k in (1, 2, 3):
        zh_copy(k).wait_send()
    for n in range(3):
        for k in range(4):
            zl_copy(n, m4(zh - k)).wait_send()

    score_scale = 1.0 / math.sqrt(HD)
    same = (iota((128, 256), 0) & 1) == (iota((128, 256), 1) & 1)

    def attend(clip):
        rows = pl.ds(clip * 128, 128)
        heads_acc[...] = jnp.zeros_like(heads_acc)

        def window_of(pair):
            d = pair // 3
            start = (3 * ((d // 2) % 2) + pair % 3) * 2 * HD
            return (d % 2, d // 4), pl.ds(start // 128 * 128, 256), start % 128

        def move(window, old, new):
            if old == new:
                return window
            return pltpu.roll(window.astype(F32), (new - old) % 256, 1).astype(BF)

        zero = jnp.zeros((128, 256), BF)
        lanes = iota((128, 256), 1)

        def by_head(window, offset):
            lane = lanes - offset
            return jnp.concatenate([
                jnp.where((lane >= 0) & (lane < HD), window, zero),
                jnp.where((lane >= HD) & (lane < 2 * HD), window, zero),
            ], axis=0)

        for i in range(H // 2):
            (qu, q_cols, q_at), (ku, k_cols, k_at), (vu, v_cols, v_at) = [window_of(n * 8 + i) for n in range(3)]
            g_at = i * 2 * HD % 128
            g_cols = pl.ds(i * 2 * HD // 128 * 128, 256)
            keys, values = pr[*ku, rows, k_cols], pr[*vu, rows, v_cols]
            queries = by_head(move(pr[*qu, rows, q_cols], q_at, k_at), k_at)
            grads = by_head(move(pr_grad[rows, g_cols], g_at, v_at), v_at)
            scores = dot(keys, queries, RHS_T) * score_scale
            e = jnp.exp(jnp.where(same, scores, -jnp.inf))
            probs = e * (1.0 / jnp.sum(e, axis=0, keepdims=True))
            grad_probs = dot(values, grads, RHS_T)
            inner = jnp.sum(probs * grad_probs, axis=0, keepdims=True)
            grad_scores = (probs * (grad_probs - inner) * score_scale).astype(BF)
            upright = jnp.concatenate([grad_scores[:, 0:128], grad_scores[:, 128:256]], axis=0)
            heads_acc[*qu, :, q_cols] += dot(upright, by_head(move(keys, k_at, q_at), q_at), LHS_T)
            heads_acc[*ku, :, k_cols] += dot(grad_scores, queries)
            heads_acc[*vu, :, v_cols] += dot(probs.astype(BF), grads)

        gp[...] = heads_acc[...].astype(BF)

    def back_rows(clip):
        by_row, by_column = [
            sum(dot(gp[core, half_of(st)], xt[core, st]) for core, st in units if (core != st) == column)
            for column in (False, True)
        ]
        gh_rows[:, 0:MAIN] = (by_row + by_columns_first(by_column)).astype(BF)
        tails = sum(
            dot(gp[core].reshape(256, 896), tail_block(core, pl.ds(0, 896)), RHS_T) for core in range(2)
        )
        gh_rows[:, MAIN:MAIN + TAIL] = tails[0:128].astype(BF)
        gh_rows[:, MAIN + TAIL:MAIN + 2 * TAIL] = tails[128:256].astype(BF)
        gh[...] = dot(gh_rows[...], table[...])

        shift_sum = jnp.sum(gh[...], axis=0, keepdims=True)
        scale_sum = jnp.sum(gh[...] * normed[clip * 128:clip * 128 + 128, :], axis=0, keepdims=True)
        for n, row in enumerate((shift_sum, scale_sum)):
            n += 2 * clip
            ms[0, n:n + 1, :] = row[:, 0:640]
            ms[0, n + 4:n + 5, 0:512] = row[:, 640:1152]
            ms[0, n + 4:n + 5, 512:640] = jnp.zeros((1, 128), F32)
        if clip == 1:
            m_start(0)

        for part in range(2):
            rows = pl.ds(clip * 128 + part * 64, 64)
            source = pl.ds(clip * 32, 32)
            grad_hidden = gh[part * 64:part * 64 + 64, :]
            nrm = normed[rows, :]
            gn = grad_hidden * (1.0 + mod_ref[1, clip:clip + 1, :])
            mean_grad = jnp.sum(gn, axis=1, keepdims=True) * (1.0 / D)
            mean_cross = jnp.sum(gn * nrm, axis=1, keepdims=True) * (1.0 / D)
            cot = rb[1, 2 * part:2 * part + 2, source, :].reshape(64, D).astype(F32)
            gt = cot + inv[rows, 0:1] * (gn - mean_grad - nrm * mean_cross)
            rr[0, 2 * part:2 * part + 2, source, :] = gt.astype(BF).reshape(2, 32, D)

        for piece in range(2):
            for k in (2, 1, 3):
                back_copy(clip, piece, k).start()
        rr.at[1, zl][clip * 32:clip * 32 + 32, :] = rr.at[0, zl][clip * 32:clip * 32 + 32, :]

    def back_copy(clip, piece, k):
        part = pl.ds(clip * 32 + piece * 16, 16)
        return copy(rr.at[0, m4(zl + k), part], rr.at[1, zl, part],
                    c_s.at[clip, piece, k], c_r.at[clip, piece, k], at_zl(k))

    def e_copy(clip, k):
        px, py = m4(x + k // 4), m4(y + lax.rem(k, 4))
        return copy(rr2.at[0, clip, px * 4 + py], rr2.at[1, clip, xy],
                    e_s.at[clip, k], e_r.at[clip, k], dev(px, py, zfull, c))

    def line_row(o):
        return ((o >> 1) & 3) * 16 + (o >> 4) * 2 + (o & 1)

    both_halves = pick(lambda o: line_row(o) + ((o >> 3) & 1) * 64, 128, 128)
    top_half = pick(lambda o: jnp.where(((o >> 3) & 1) == 0, line_row(o), -1), 128, 64)

    def plane_start(clip):
        for piece in range(2):
            for k in (1, 2, 3):
                back_copy(clip, piece, k).wait()
            source = pl.ds(clip * 32 + piece * 16, 16)
            to = pl.ds(piece * 8, 8)
            block = rr[1, :, source, :].reshape(64, D)
            stacked = jnp.concatenate([block[:, 0:512], block[:, 640:1152]], axis=0)
            rr2[0, clip, to, :, 0:512] = dot(both_halves, stacked).astype(BF).reshape(8, 16, 512)
            rr2[0, clip, to, :, 512:640] = dot(top_half, block[:, 512:640]).astype(BF).reshape(8, 16, 128)
            for a in range(2):
                i = m4(2 * piece + a - x)
                for j in (2, 1, 3):
                    e_copy(clip, i * 4 + j).start()

                @pl.when(i != 0)
                def _(i=i):
                    e_copy(clip, i * 4).start()

        rr2[1, clip, xy] = rr2[0, clip, xy]

    upper = pick(lambda o: (o >> 3) * 16 + (o & 7), 128, 256)
    lower = pick(lambda o: (o >> 3) * 16 + 8 + (o & 7), 128, 256)

    def finish(clip):
        for k in range(1, 16):
            e_copy(clip, k).wait()

        rows = rr2[1, clip].reshape(256, 640)
        out[clip, :, 0:640] = dot(upper, rows).astype(BF)
        out[clip, :, 640:1152] = dot(lower, rows[:, 0:512]).astype(BF)
        cp = pltpu.make_async_copy(out.at[clip], out_hbm.at[clip], out_sem.at[clip])
        cp.start()
        return cp

    places = (zl, x, y)

    def m_copy(step, k):
        to = (at_zl(k), dev(m4(x + k), y, zfull, c), dev(x, m4(y + k), zfull, c))[step]
        return copy(ms.at[step], mr.at[step, places[step]], m_s.at[step, k], m_r.at[step, k], to)

    def m_start(step):
        for k in (1, 2, 3):
            m_copy(step, k).start()
        mr[step, places[step]] = ms[step]

    def m_sum(step):
        for k in (1, 2, 3):
            m_copy(step, k).wait()
        return ((mr[step, 0] + mr[step, 1]) + mr[step, 2]) + mr[step, 3]

    attend(0)
    back_rows(0)
    attend(1)
    plane_start(0)
    back_rows(1)
    ms[1] = m_sum(0)
    m_start(1)
    stored_first = finish(0)
    ms[2] = m_sum(1)
    m_start(2)
    plane_start(1)
    total = m_sum(2)
    for clip in range(2):
        outm_ref[clip, :, 0:640] = total[2 * clip:2 * clip + 2]
        outm_ref[clip, :, 640:1152] = total[4 + 2 * clip:6 + 2 * clip, 0:512]
    stored_second = finish(1)
    stored_first.wait()
    stored_second.wait()


def local(tokens, modulation, cotangent, qkv_weight, out_weight):
    table = jnp.asarray(place_table(), BF)
    hbm = pl.BlockSpec(memory_space=pl.ANY)
    dma = pltpu.SemaphoreType.DMA
    vmem = pltpu.VMEM
    grad_tokens, grad_modulation = pl.pallas_call(
        kernel,
        out_shape=(
            jax.ShapeDtypeStruct((2, 128, D), BF),
            jax.ShapeDtypeStruct((2, 2, D), F32),
        ),
        in_specs=[hbm] * 6,
        out_specs=(hbm, pl.BlockSpec(memory_space=pltpu.VMEM)),
        scratch_shapes=[
            vmem((2, 2, 128, D), BF),
            vmem((3, 2, D), F32),
            vmem((18, 432), BF),
            vmem((18, 144), BF),
            vmem((2, 16, 16, D), BF),
            vmem((2, 16, 16, D), BF),
            vmem((2, 4, 64, D), BF),
            vmem((2, 4, 64, D), BF),
            vmem((4, 4, 16, 768), BF),
            vmem((2, 2, 4, 4, 80, D), BF),
            vmem((2, 2, 896, MAIN), BF),
            vmem((MAIN + 2 * TAIL, D), BF),
            vmem((256, D), BF),
            vmem((4, 2, 256, 256), BF),
            vmem((2, 256, TAIL), BF),
            vmem((2, 2, 256, 384), BF),
            vmem((256, D), F32),
            vmem((256, 128), F32),
            vmem((2, 2, 256, 896), F32),
            vmem((2, 256, MAIN), F32),
            vmem((2, 2, 256, 896), BF),
            vmem((256, D), BF),
            vmem((2, 2, 128, 896), F32),
            vmem((2, 2, 128, 896), BF),
            vmem((128, MAIN + 2 * TAIL), BF),
            vmem((128, D), F32),
            vmem((2, 4, 64, D), BF),
            vmem((2, 2, 16, 16, 640), BF),
            vmem((2, 128, D), BF),
            vmem((3, 8, 640), F32),
            vmem((3, 4, 8, 640), F32),
            dma((6,)), dma((2,)),
            dma((4,)), dma((4,)), dma((3, 4)), dma((3, 4)),
            dma((2, 16)), dma((2, 16)), dma((2, 16)), dma((2, 16)),
            dma((2, 16)), dma((2, 16)), dma((2, 4)), dma((2, 4)),
            dma((2, 2, 4)), dma((2, 2, 4)), dma((2, 16)), dma((2, 16)),
            dma((3, 4)), dma((3, 4)),
        ],
        compiler_params=pltpu.CompilerParams(
            collective_id=0, has_side_effects=True, vmem_limit_bytes=60 * 1024 * 1024
        ),
        name="sublayer_backward",
    )(
        tokens.reshape(2, 128, D), modulation.transpose(1, 0, 2), cotangent.reshape(2, 128, D),
        qkv_weight, out_weight, table,
    )
    return grad_tokens.reshape(2, 1, 128, D), grad_modulation


def solution(mesh):
    in_specs = (
        P("dp", "seq", None, None),
        P("dp", None, None),
        P("dp", "seq", None, None),
        P("seq", "dp"),
        P("seq", "dp"),
    )
    out_specs = (P("dp", "seq", None, None), P("dp", None, None))
    return jax.shard_map(local, mesh=mesh, in_specs=in_specs, out_specs=out_specs, check_vma=False)
```

```python
import functools
import math

import jax
import jax.numpy as jnp
import numpy as np
from jax import lax
from jax.experimental import pallas as pl
from jax.experimental.pallas import tpu as pltpu
from jax.sharding import PartitionSpec as P

D = 1152
H = 16
HD = 72
EPS = 1e-06
MESH = pl.DeviceIdType.MESH
BF = jnp.bfloat16
F32 = jnp.float32
RHS_T = (((1,), (1,)), ((), ()))
LHS_T = (((0,), (0,)), ((), ()))


MAIN, TAIL = 1024, 256


def place_table():
    table = np.zeros((MAIN + 2 * TAIL, D), np.float32)
    for feature in range(D):
        zl, rest = divmod(feature, 288)
        position, i = divmod(rest, 18)
        t = zl * 18 + i
        if t < 64:
            table[position * 64 + t, feature] = 1
        else:
            table[MAIN + position * 16 + t - 64, feature] = 1
            table[MAIN + TAIL + position * 16 + 8 + t - 64, feature] = 1
    return table


def dot(a, b, dims=(((1,), (0,)), ((), ()))):
    return lax.dot_general(a, b, dims, preferred_element_type=F32)


def iota(shape, dim):
    return lax.broadcasted_iota(jnp.int32, shape, dim)


def pick(source_row, n=256, m=256):
    return (source_row(iota((n, m), 0)) == iota((n, m), 1)).astype(F32).astype(BF)


def kernel(
    tok_hbm, mod_hbm, cot_hbm, wq_hbm, wo_hbm, table_hbm,
    out_hbm, outm_ref,
    raw, mod_ref, wq_ref, wo_ref,
    sa, ra, sb, rb, z, xs, xt, table, hid, hidg, hidt, gated, normed, inv, acc, acc_grad, pr, pr_grad, heads_acc, gp, gh_rows, gh, rr, rr2, out, ms, mr,
    in_sem, out_sem, zh_s, zh_r, zl_s, zl_r, w_s, w_r, wc_s, wc_r,
    a_s, a_r, b_s, b_r, c_s, c_r, e_s, e_r, m_s, m_r,
):
    s, q = lax.axis_index("seq"), lax.axis_index("dp")
    y, x, zl = lax.rem(s, 4), lax.rem(s // 4, 4), s // 16
    zh, c = q // 2, lax.rem(q, 2)
    xy = x * 4 + y
    zfull = zh * 4 + zl

    def m4(v):
        return lax.rem(v + 8, 4)

    def dev(x_, y_, z_, c_):
        return ((lax.rem(z_, 4) * 4 + x_) * 4 + y_, (z_ // 4) * 2 + c_)

    def at_xy(k):
        return dev(m4(x + k // 4), m4(y + lax.rem(k, 4)), zfull, c)

    def at_zl(k):
        return dev(x, y, zh * 4 + m4(zl + k), c)

    def at_zh(k):
        return dev(x, y, m4(zh + k) * 4 + zl, c)

    def at_ring(k):
        return dev(x, y, lax.rem(zfull + k + 16, 16), c)

    other = dev(x, y, zfull, 1 - c)

    def copy(src, dst, ss, rs, to):
        return pltpu.make_async_remote_copy(
            src_ref=src, dst_ref=dst, send_sem=ss, recv_sem=rs, device_id=to, device_id_type=MESH
        )

    loads = [
        pltpu.make_async_copy(src, dst, in_sem.at[n])
        for n, (src, dst) in enumerate((
            (wq_hbm, wq_ref), (wo_hbm, wo_ref), (tok_hbm, raw.at[0]), (cot_hbm, raw.at[1]),
            (mod_hbm, mod_ref), (table_hbm, table),
        ))
    ]
    for load in loads:
        load.start()

    barrier = pltpu.get_barrier_semaphore()

    def greet(to):
        pl.semaphore_signal(barrier, inc=1, device_id=to, device_id_type=MESH)

    for k in (1, 2, 3):
        greet(at_zh(k))
        greet(at_zl(k))
    for k in (1, -1, 2, -2):
        greet(at_ring(k))
    greet(other)

    for k in range(1, 16):
        greet(at_xy(k))

    loads[0].wait()
    loads[1].wait()
    wide = jnp.concatenate(
        [wq_ref[...].astype(F32), wo_ref[...].astype(F32), jnp.zeros((18, 64), F32)], axis=1
    )
    ends = [wide[16 + j:17 + j, 128 * m:128 * m + 128] for j in range(2) for m in range(5)]
    ends = jnp.concatenate(ends + [jnp.zeros((6, 128), F32)], axis=0)
    z[zl, zh] = jnp.concatenate([wide[:16], ends], axis=1).astype(BF)

    to_plane = pick(lambda o: ((o >> 3) & 1) * 128 + (o >> 4) * 8 + (o & 7))

    def first_order(n):
        loads[2 + n].wait()
        sa[n] = dot(to_plane, raw[n].reshape(256, D)).astype(BF).reshape(16, 16, D)

    first_order(0)
    pl.semaphore_wait(barrier, 26)

    def zh_copy(k):
        ref = z.at[zl, zh]
        return copy(ref, ref, zh_s.at[k], zh_r.at[k], at_zh(k))

    ring = (1, -1, 2)

    def zl_copy(n, group):
        ref = z.at[zl, group]
        return copy(ref, ref, zl_s.at[n, group], zl_r.at[n, group], at_ring(ring[n]))

    def zl_arrived(n, group):
        ref = z.at[m4(zl - ring[n]), group]
        copy(ref, ref, zl_s.at[n, group], zl_r.at[n, group], at_ring(ring[n])).wait_recv()

    for k in (2, 1, 3):
        zh_copy(k).start()
    for n in range(3):
        zl_copy(n, zh).start()

    def a_copy(n, k):
        return copy(sa.at[n, m4(x + k // 4) * 4 + m4(y + lax.rem(k, 4))], ra.at[n, xy],
                    a_s.at[n, k], a_r.at[n, k], at_xy(k))

    def a_send(n):
        for k in (10, 8, 2, 9, 11, 6, 14, 5, 7, 13, 15, 4, 12, 1, 3):
            a_copy(n, k).start()

        ra[n, xy] = sa[n, xy]

    a_send(0)
    first_order(1)
    a_send(1)

    for k in (1, 3, 2):
        zh_copy(k).wait_recv()
        for n in range(3):
            zl_copy(n, m4(zh - k)).start()

    def b_copy(n, k):
        return copy(sb.at[n, m4(zl + k)], rb.at[n, zl], b_s.at[n, k], b_r.at[n, k], at_zl(k))

    to_line = pick(lambda o: ((o >> 1) & 15) * 16 + ((o >> 5) & 1) * 8 + (o >> 6) * 2 + (o & 1))

    def second_step(n):
        for k in range(1, 16):
            a_copy(n, k).wait()

        sb[n] = dot(to_line, ra[n].reshape(256, D)).astype(BF).reshape(4, 64, D)
        for k in (2, 1, 3):
            b_copy(n, k).start()
        rb[n, zl] = sb[n, zl]

    mine = zh // 2

    def rows_of(group):
        parts = []
        for k in range(4):
            stored = z[k, group].astype(F32)
            parts.append(stored[:, :640])
            for j in range(2):
                parts.append(jnp.concatenate(
                    [stored[5 * j + m:5 * j + m + 1, 640:768] for m in range(5)], axis=1
                ))
        return jnp.concatenate(parts, axis=0)

    def unit(half):
        for n in range(3):
            for b in range(2):
                zl_arrived(n, 2 * half + b)
        a, b = rows_of(2 * half), rows_of(2 * half + 1)
        return jnp.concatenate([a[:, :432], b[:, :432], a[:, 432:576], b[:, 432:576]], axis=1)

    first_axis = ((c, (1 - c)), ((1 - c), c))

    def shifted(st, i, j):
        fx, fy = first_axis[st]
        return m4(x + i * fx + j * fy), m4(y + i * fy + j * fx)

    def block_of(core, st, px, py):
        return xs.at[core, st, px, py, pl.ds(0, 64)] if st == 0 else xs.at[core, st, px, py]

    def held(st, i, j):
        px, py = shifted(st, i, j)
        return block_of(c, st, px, py)

    sent = []

    def w_send(st, i, j, to_i, to_j):
        ref = held(st, i, j)
        px, py = shifted(st, to_i, to_j)
        index = ((i - to_i) % 4) * 4 + (j - to_j) % 4
        cp = copy(ref, ref, w_s.at[st, index], w_r.at[st, index], dev(px, py, zfull, c))
        cp.start()
        sent.append(cp)

    def w_over(st, i, j):
        ref = held(st, i, j)
        index = i * 4 + j
        cp = copy(ref, ref, wc_s.at[st, index], wc_r.at[st, index], other)
        cp.start()
        sent.append(cp)

    def w_arrived(st, i, j):
        ref = held(st, i, j)
        index = i * 4 + j
        copy(ref, ref, w_s.at[st, index], w_r.at[st, index], other).wait_recv()
        w_over(st, i, j)

    def w_both_ways(st, i):
        w_send(st, i, 0, 0, 1)
        w_send(st, i, 0, 0, -1)

    def w_sides(st, i):
        w_arrived(st, i, 3)
        if i in (0, 2):
            w_send(st, i, 3, 0, 1)
        w_arrived(st, i, 1)
        if i in (1, 3):
            w_send(st, i, 1, 0, -1)

    def w_first(st):
        for i in (1, -1):
            w_send(st, 0, 0, i, 0)
        w_both_ways(st, 0)
        w_over(st, 0, 0)

    second_step(0)
    near = unit(mine)
    xs[c, 0, x, y, 0:64, :] = near[:64].astype(BF)
    w_first(0)
    far = unit(1 - mine)
    xs[c, 1, x, y, 0:64, :] = far[:64].astype(BF)
    xs[c, 1, x, y, 64:80, :] = jnp.concatenate([
        jnp.where(mine == 0, near[64:], far[64:]), jnp.where(mine == 0, far[64:], near[64:])
    ], axis=0).astype(BF)
    w_first(1)
    second_step(1)
    for i in (1, 3):
        for st in range(2):
            w_arrived(st, i, 0)
            if (st, i) in ((0, 3), (1, 1)):
                w_send(st, i, 0, 1 if i == 3 else -1, 0)
            w_both_ways(st, i)
    for st in range(2):
        w_sides(st, 0)
    for st in range(2):
        w_arrived(st, 2, 0)
        w_both_ways(st, 2)

    def places_of(i):
        clip, lines = lax.rem(i, 2), pl.ds(pl.multiple_of(i // 2 * 2, 2), 2)
        rows = pl.ds(pl.multiple_of(clip * 128 + i // 2 * 64, 64), 64)
        return clip, lines, rows, pl.ds(pl.multiple_of(clip * 32, 32), 32)

    def norm_rows(i):
        clip, lines, rows, source = places_of(i)
        tile = rb[0, lines, source, :].reshape(64, D).astype(F32)
        mean = jnp.sum(tile, axis=1, keepdims=True) * (1.0 / D)
        centred = tile - mean
        inv_std = lax.rsqrt(jnp.sum(centred * centred, axis=1, keepdims=True) * (1.0 / D) + EPS)
        nrm = centred * inv_std
        normed[rows, :] = nrm
        inv[rows, :] = jnp.broadcast_to(inv_std, (64, 128))
        hid[rows, :] = (nrm * (1.0 + mod_ref[1, pl.ds(clip, 1), :]) + mod_ref[0, pl.ds(clip, 1), :]).astype(BF)

    def gate_rows(i):
        clip, lines, rows, source = places_of(i)
        cot = rb[1, lines, source, :].reshape(64, D).astype(F32)
        g = (cot * mod_ref[2, pl.ds(clip, 1), :]).astype(BF).astype(F32)
        for core in range(2):
            for half in range(2):
                d = 4 * half + core
                gated[core, half, rows, :] = jnp.concatenate([
                    jnp.zeros((64, 96), F32), g[:, 144 * d:144 * d + 144], g[:, 144 * d + 288:144 * d + 432]
                ], axis=1).astype(BF)

    def hidden_in(places):
        return dot(hid[...], places, RHS_T).astype(BF)

    def table_column(yj):
        return jnp.concatenate(
            [table[pl.ds(pl.multiple_of((k * 4 + yj) * 64, 64), 64), :] for k in range(4)], axis=0
        )

    def table_row(xj):
        return table[pl.ds(pl.multiple_of(xj * 256, 256), 256), :]

    def main_block(core, st, j, cols):
        if core != st:
            return xs[core, st, :, m4(y + j), 0:64, cols].reshape(256, -1)
        return xs[core, st, m4(x + j), :, 0:64, cols].reshape(256, -1)

    def tail_block(core, cols):
        return xs[core, 1, :, :, 64:80, cols].reshape(TAIL, -1)

    units = [(core, st) for core in range(2) for st in range(2)]

    def half_of(st):
        return lax.rem(mine + st, 2)

    def project(j, last=False):
        for core, st in units:
            for cols in (pl.ds(0, 512), pl.ds(512, 384)):
                now = dot(hidg[j, 0 if core != st else 1], main_block(core, st, j, cols))
                if j == 0:
                    acc[core, st, :, cols] = now
                elif not last:
                    acc[core, st, :, cols] += now
                else:
                    tail = dot(hidt[half_of(st)], tail_block(core, cols))
                    pr[core, half_of(st), :, cols] = (acc[core, st, :, cols] + now + tail).astype(BF)

    def by_columns_first(part):
        return jnp.concatenate([
            part[:, (b * 4 + a) * 64:(b * 4 + a) * 64 + 64] for a in range(4) for b in range(4)
        ], axis=1)

    def lanes_of(column, j):
        at = m4(y + j) if column else m4(x + j)
        return pl.ds(pl.multiple_of(at * 256, 256), 256)

    def upright_rows(j):
        for core, st in units:
            xt[core, st, :, lanes_of(core != st, j)] = main_block(core, st, j, pl.ds(0, 896)).T

    out_cols = pl.ds(768, 384)

    def project_grad(j):
        for column in (True, False):
            acc_grad[int(column), :, lanes_of(column, j)] = sum(
                dot(gated[core, half_of(st)], main_block(core, st, j, out_cols), RHS_T)
                for core, st in units if (core != st) == column
            )

    def place_grad():
        main = (acc_grad[0] + by_columns_first(acc_grad[1])).astype(BF)
        first, second = [
            sum(dot(gated[core, half], tail_block(core, out_cols), RHS_T) for core in range(2)) for half in range(2)
        ]
        ends = (first + pltpu.roll(second, TAIL - 8, 1)).astype(BF)
        pr_grad[...] = (dot(main, table[0:MAIN, :]) + dot(ends, table[MAIN:MAIN + TAIL, :])).astype(BF)

    def w_across(i, j):
        for st in range(2):
            px, py = shifted(1 - st, i, j)
            ref = block_of(1 - c, st, px, py)
            index = i * 4 + j
            copy(ref, ref, wc_s.at[st, index], wc_r.at[st, index], other).wait_recv()

    for k in (1, 2, 3):
        b_copy(0, k).wait()
    for load in loads[4:]:
        load.wait()
    pl.loop(0, 4)(norm_rows)
    for k in range(2):
        hidt[k] = hidden_in(table[MAIN + k * TAIL:MAIN + (k + 1) * TAIL, :])
    for j in range(4):
        hidg[j, 0] = hidden_in(table_column(m4(y + j)))
        hidg[j, 1] = hidden_in(table_row(m4(x + j)))
    for st in range(2):
        w_sides(st, 1)
    for i in range(4):
        w_across(i, 0)
    project(0)
    upright_rows(0)
    for i in (3, 2):
        for st in range(2):
            w_sides(st, i)
    for j in (3, 1):
        for i in range(4):
            w_across(i, j)
        project(j)
        upright_rows(j)
    for k in (1, 2, 3):
        b_copy(1, k).wait()
    pl.loop(0, 4)(gate_rows)
    for j in (0, 3, 1):
        project_grad(j)
    for i in range(4):
        for st in range(2):
            w_arrived(st, i, 2)
    for i in range(4):
        w_across(i, 2)
    project(2, last=True)
    project_grad(2)
    place_grad()
    upright_rows(2)
    for cp in sent:
        cp.wait_send()
    for k in (1, 2, 3):
        zh_copy(k).wait_send()
    for n in range(3):
        for k in range(4):
            zl_copy(n, m4(zh - k)).wait_send()

    score_scale = 1.0 / math.sqrt(HD)
    same = (iota((128, 256), 0) & 1) == (iota((128, 256), 1) & 1)

    def attend(clip):
        rows = pl.ds(clip * 128, 128)
        heads_acc[...] = jnp.zeros_like(heads_acc)

        def window_of(pair):
            d = pair // 3
            start = (3 * ((d // 2) % 2) + pair % 3) * 2 * HD
            return (d % 2, d // 4), pl.ds(start // 128 * 128, 256), start % 128

        def move(window, old, new):
            if old == new:
                return window
            return pltpu.roll(window.astype(F32), (new - old) % 256, 1).astype(BF)

        zero = jnp.zeros((128, 256), BF)
        lanes = iota((128, 256), 1)

        def by_head(window, offset):
            lane = lanes - offset
            return jnp.concatenate([
                jnp.where((lane >= 0) & (lane < HD), window, zero),
                jnp.where((lane >= HD) & (lane < 2 * HD), window, zero),
            ], axis=0)

        for i in range(H // 2):
            (qu, q_cols, q_at), (ku, k_cols, k_at), (vu, v_cols, v_at) = [window_of(n * 8 + i) for n in range(3)]
            g_at = i * 2 * HD % 128
            g_cols = pl.ds(i * 2 * HD // 128 * 128, 256)
            keys, values = pr[*ku, rows, k_cols], pr[*vu, rows, v_cols]
            queries = by_head(move(pr[*qu, rows, q_cols], q_at, k_at), k_at)
            grads = by_head(move(pr_grad[rows, g_cols], g_at, v_at), v_at)
            scores = dot(keys, queries, RHS_T) * score_scale
            e = jnp.exp(jnp.where(same, scores, -jnp.inf))
            probs = e * (1.0 / jnp.sum(e, axis=0, keepdims=True))
            grad_probs = dot(values, grads, RHS_T)
            inner = jnp.sum(probs * grad_probs, axis=0, keepdims=True)
            grad_scores = (probs * (grad_probs - inner) * score_scale).astype(BF)
            upright = jnp.concatenate([grad_scores[:, 0:128], grad_scores[:, 128:256]], axis=0)
            heads_acc[*qu, :, q_cols] += dot(upright, by_head(move(keys, k_at, q_at), q_at), LHS_T)
            heads_acc[*ku, :, k_cols] += dot(grad_scores, queries)
            heads_acc[*vu, :, v_cols] += dot(probs.astype(BF), grads)

        gp[...] = heads_acc[...].astype(BF)

    def back_rows(clip):
        by_row, by_column = [
            sum(dot(gp[core, half_of(st)], xt[core, st]) for core, st in units if (core != st) == column)
            for column in (False, True)
        ]
        gh_rows[:, 0:MAIN] = (by_row + by_columns_first(by_column)).astype(BF)
        tails = sum(
            dot(gp[core].reshape(256, 896), tail_block(core, pl.ds(0, 896)), RHS_T) for core in range(2)
        )
        gh_rows[:, MAIN:MAIN + TAIL] = tails[0:128].astype(BF)
        gh_rows[:, MAIN + TAIL:MAIN + 2 * TAIL] = tails[128:256].astype(BF)
        gh[...] = dot(gh_rows[...], table[...])

        shift_sum = jnp.sum(gh[...], axis=0, keepdims=True)
        scale_sum = jnp.sum(gh[...] * normed[clip * 128:clip * 128 + 128, :], axis=0, keepdims=True)
        for n, row in enumerate((shift_sum, scale_sum)):
            n += 2 * clip
            ms[0, n:n + 1, :] = row[:, 0:640]
            ms[0, n + 4:n + 5, 0:512] = row[:, 640:1152]
            ms[0, n + 4:n + 5, 512:640] = jnp.zeros((1, 128), F32)
        if clip == 1:
            m_start(0)

        for part in range(2):
            rows = pl.ds(clip * 128 + part * 64, 64)
            source = pl.ds(clip * 32, 32)
            grad_hidden = gh[part * 64:part * 64 + 64, :]
            nrm = normed[rows, :]
            gn = grad_hidden * (1.0 + mod_ref[1, clip:clip + 1, :])
            mean_grad = jnp.sum(gn, axis=1, keepdims=True) * (1.0 / D)
            mean_cross = jnp.sum(gn * nrm, axis=1, keepdims=True) * (1.0 / D)
            cot = rb[1, 2 * part:2 * part + 2, source, :].reshape(64, D).astype(F32)
            gt = cot + inv[rows, 0:1] * (gn - mean_grad - nrm * mean_cross)
            rr[0, 2 * part:2 * part + 2, source, :] = gt.astype(BF).reshape(2, 32, D)

        for piece in range(2):
            for k in (2, 1, 3):
                back_copy(clip, piece, k).start()
        rr.at[1, zl][clip * 32:clip * 32 + 32, :] = rr.at[0, zl][clip * 32:clip * 32 + 32, :]

    def back_copy(clip, piece, k):
        part = pl.ds(clip * 32 + piece * 16, 16)
        return copy(rr.at[0, m4(zl + k), part], rr.at[1, zl, part],
                    c_s.at[clip, piece, k], c_r.at[clip, piece, k], at_zl(k))

    def e_copy(clip, k):
        px, py = m4(x + k // 4), m4(y + lax.rem(k, 4))
        return copy(rr2.at[0, clip, px * 4 + py], rr2.at[1, clip, xy],
                    e_s.at[clip, k], e_r.at[clip, k], dev(px, py, zfull, c))

    def line_row(o):
        return ((o >> 1) & 3) * 16 + (o >> 4) * 2 + (o & 1)

    both_halves = pick(lambda o: line_row(o) + ((o >> 3) & 1) * 64, 128, 128)
    top_half = pick(lambda o: jnp.where(((o >> 3) & 1) == 0, line_row(o), -1), 128, 64)

    def plane_start(clip):
        for piece in range(2):
            for k in (1, 2, 3):
                back_copy(clip, piece, k).wait()
            source = pl.ds(clip * 32 + piece * 16, 16)
            to = pl.ds(piece * 8, 8)
            block = rr[1, :, source, :].reshape(64, D)
            stacked = jnp.concatenate([block[:, 0:512], block[:, 640:1152]], axis=0)
            rr2[0, clip, to, :, 0:512] = dot(both_halves, stacked).astype(BF).reshape(8, 16, 512)
            rr2[0, clip, to, :, 512:640] = dot(top_half, block[:, 512:640]).astype(BF).reshape(8, 16, 128)
            for a in range(2):
                i = m4(2 * piece + a - x)
                for j in (2, 1, 3):
                    e_copy(clip, i * 4 + j).start()

                @pl.when(i != 0)
                def _(i=i):
                    e_copy(clip, i * 4).start()

        rr2[1, clip, xy] = rr2[0, clip, xy]

    upper = pick(lambda o: (o >> 3) * 16 + (o & 7), 128, 256)
    lower = pick(lambda o: (o >> 3) * 16 + 8 + (o & 7), 128, 256)

    def finish(clip):
        for k in range(1, 16):
            e_copy(clip, k).wait()

        rows = rr2[1, clip].reshape(256, 640)
        out[clip, :, 0:640] = dot(upper, rows).astype(BF)
        out[clip, :, 640:1152] = dot(lower, rows[:, 0:512]).astype(BF)
        cp = pltpu.make_async_copy(out.at[clip], out_hbm.at[clip], out_sem.at[clip])
        cp.start()
        return cp

    places = (zl, x, y)

    def m_copy(step, k):
        to = (at_zl(k), dev(m4(x + k), y, zfull, c), dev(x, m4(y + k), zfull, c))[step]
        return copy(ms.at[step], mr.at[step, places[step]], m_s.at[step, k], m_r.at[step, k], to)

    def m_start(step):
        for k in (1, 2, 3):
            m_copy(step, k).start()
        mr[step, places[step]] = ms[step]

    def m_sum(step):
        for k in (1, 2, 3):
            m_copy(step, k).wait()
        return ((mr[step, 0] + mr[step, 1]) + mr[step, 2]) + mr[step, 3]

    attend(0)
    back_rows(0)
    attend(1)
    plane_start(0)
    back_rows(1)
    ms[1] = m_sum(0)
    m_start(1)
    stored_first = finish(0)
    ms[2] = m_sum(1)
    m_start(2)
    plane_start(1)
    total = m_sum(2)
    for clip in range(2):
        outm_ref[clip, :, 0:640] = total[2 * clip:2 * clip + 2]
        outm_ref[clip, :, 640:1152] = total[4 + 2 * clip:6 + 2 * clip, 0:512]
    stored_second = finish(1)
    stored_first.wait()
    stored_second.wait()


def local(tokens, modulation, cotangent, qkv_weight, out_weight):
    table = jnp.asarray(place_table(), BF)
    hbm = pl.BlockSpec(memory_space=pl.ANY)
    dma = pltpu.SemaphoreType.DMA
    vmem = pltpu.VMEM
    grad_tokens, grad_modulation = pl.pallas_call(
        kernel,
        out_shape=(
            jax.ShapeDtypeStruct((2, 128, D), BF),
            jax.ShapeDtypeStruct((2, 2, D), F32),
        ),
        in_specs=[hbm] * 6,
        out_specs=(hbm, pl.BlockSpec(memory_space=pltpu.VMEM)),
        scratch_shapes=[
            vmem((2, 2, 128, D), BF),
            vmem((3, 2, D), F32),
            vmem((18, 432), BF),
            vmem((18, 144), BF),
            vmem((2, 16, 16, D), BF),
            vmem((2, 16, 16, D), BF),
            vmem((2, 4, 64, D), BF),
            vmem((2, 4, 64, D), BF),
            vmem((4, 4, 16, 768), BF),
            vmem((2, 2, 4, 4, 80, D), BF),
            vmem((2, 2, 896, MAIN), BF),
            vmem((MAIN + 2 * TAIL, D), BF),
            vmem((256, D), BF),
            vmem((4, 2, 256, 256), BF),
            vmem((2, 256, TAIL), BF),
            vmem((2, 2, 256, 384), BF),
            vmem((256, D), F32),
            vmem((256, 128), F32),
            vmem((2, 2, 256, 896), F32),
            vmem((2, 256, MAIN), F32),
            vmem((2, 2, 256, 896), BF),
            vmem((256, D), BF),
            vmem((2, 2, 128, 896), F32),
            vmem((2, 2, 128, 896), BF),
            vmem((128, MAIN + 2 * TAIL), BF),
            vmem((128, D), F32),
            vmem((2, 4, 64, D), BF),
            vmem((2, 2, 16, 16, 640), BF),
            vmem((2, 128, D), BF),
            vmem((3, 8, 640), F32),
            vmem((3, 4, 8, 640), F32),
            dma((6,)), dma((2,)),
            dma((4,)), dma((4,)), dma((3, 4)), dma((3, 4)),
            dma((2, 16)), dma((2, 16)), dma((2, 16)), dma((2, 16)),
            dma((2, 16)), dma((2, 16)), dma((2, 4)), dma((2, 4)),
            dma((2, 2, 4)), dma((2, 2, 4)), dma((2, 16)), dma((2, 16)),
            dma((3, 4)), dma((3, 4)),
        ],
        compiler_params=pltpu.CompilerParams(
            collective_id=0, has_side_effects=True, vmem_limit_bytes=60 * 1024 * 1024
        ),
        name="sublayer_backward",
    )(
        tokens.reshape(2, 128, D), modulation.transpose(1, 0, 2), cotangent.reshape(2, 128, D),
        qkv_weight, out_weight, table,
    )
    return grad_tokens.reshape(2, 1, 128, D), grad_modulation


def solution(mesh):
    in_specs = (
        P("dp", "seq", None, None),
        P("dp", None, None),
        P("dp", "seq", None, None),
        P("seq", "dp"),
        P("seq", "dp"),
    )
    out_specs = (P("dp", "seq", None, None), P("dp", None, None))
    return jax.shard_map(local, mesh=mesh, in_specs=in_specs, out_specs=out_specs, check_vma=False)
```

```python
import functools
import math

import jax
import jax.numpy as jnp
import numpy as np
from jax import lax
from jax.experimental import pallas as pl
from jax.experimental.pallas import tpu as pltpu
from jax.sharding import PartitionSpec as P

D = 1152
H = 16
HD = 72
EPS = 1e-06
MESH = pl.DeviceIdType.MESH
BF = jnp.bfloat16
F32 = jnp.float32
RHS_T = (((1,), (1,)), ((), ()))
LHS_T = (((0,), (0,)), ((), ()))


MAIN, TAIL = 1024, 256


def place_table():
    table = np.zeros((MAIN + 2 * TAIL, D), np.float32)
    for feature in range(D):
        zl, rest = divmod(feature, 288)
        position, i = divmod(rest, 18)
        t = zl * 18 + i
        if t < 64:
            table[position * 64 + t, feature] = 1
        else:
            table[MAIN + position * 16 + t - 64, feature] = 1
            table[MAIN + TAIL + position * 16 + 8 + t - 64, feature] = 1
    return table


def dot(a, b, dims=(((1,), (0,)), ((), ()))):
    return lax.dot_general(a, b, dims, preferred_element_type=F32)


def iota(shape, dim):
    return lax.broadcasted_iota(jnp.int32, shape, dim)


def pick(source_row, n=256, m=256):
    return (source_row(iota((n, m), 0)) == iota((n, m), 1)).astype(F32).astype(BF)


def kernel(
    tok_hbm, mod_hbm, cot_hbm, wq_hbm, wo_hbm, table_hbm,
    out_hbm, outm_ref,
    raw, mod_ref, wq_ref, wo_ref,
    sa, ra, sb, rb, z, xs, xt, table, hid, hidg, hidt, gated, normed, inv, acc, acc_grad, pr, pr_grad, heads_acc, gp, gh_rows, gh, rr, rr2, out, ms, mr,
    in_sem, out_sem, zh_s, zh_r, zl_s, zl_r, w_s, w_r, wc_s, wc_r,
    a_s, a_r, b_s, b_r, c_s, c_r, e_s, e_r, m_s, m_r,
):
    s, q = lax.axis_index("seq"), lax.axis_index("dp")
    y, x, zl = lax.rem(s, 4), lax.rem(s // 4, 4), s // 16
    zh, c = q // 2, lax.rem(q, 2)
    xy = x * 4 + y
    zfull = zh * 4 + zl

    def m4(v):
        return lax.rem(v + 8, 4)

    def dev(x_, y_, z_, c_):
        return ((lax.rem(z_, 4) * 4 + x_) * 4 + y_, (z_ // 4) * 2 + c_)

    def at_xy(k):
        return dev(m4(x + k // 4), m4(y + lax.rem(k, 4)), zfull, c)

    def at_zl(k):
        return dev(x, y, zh * 4 + m4(zl + k), c)

    def at_zh(k):
        return dev(x, y, m4(zh + k) * 4 + zl, c)

    def at_ring(k):
        return dev(x, y, lax.rem(zfull + k + 16, 16), c)

    other = dev(x, y, zfull, 1 - c)

    def copy(src, dst, ss, rs, to):
        return pltpu.make_async_remote_copy(
            src_ref=src, dst_ref=dst, send_sem=ss, recv_sem=rs, device_id=to, device_id_type=MESH
        )

    loads = [
        pltpu.make_async_copy(src, dst, in_sem.at[n])
        for n, (src, dst) in enumerate((
            (wq_hbm, wq_ref), (wo_hbm, wo_ref), (tok_hbm, raw.at[0]), (cot_hbm, raw.at[1]),
            (mod_hbm, mod_ref), (table_hbm, table),
        ))
    ]
    for load in loads:
        load.start()

    barrier = pltpu.get_barrier_semaphore()

    def greet(to):
        pl.semaphore_signal(barrier, inc=1, device_id=to, device_id_type=MESH)

    for k in (1, 2, 3):
        greet(at_zh(k))
        greet(at_zl(k))
    for k in (1, -1, 2, -2):
        greet(at_ring(k))
    greet(other)

    for k in range(1, 16):
        greet(at_xy(k))

    loads[0].wait()
    loads[1].wait()
    wide = jnp.concatenate(
        [wq_ref[...].astype(F32), wo_ref[...].astype(F32), jnp.zeros((18, 64), F32)], axis=1
    )
    ends = [wide[16 + j:17 + j, 128 * m:128 * m + 128] for j in range(2) for m in range(5)]
    ends = jnp.concatenate(ends + [jnp.zeros((6, 128), F32)], axis=0)
    z[zl, zh] = jnp.concatenate([wide[:16], ends], axis=1).astype(BF)

    to_plane = pick(lambda o: ((o >> 3) & 1) * 128 + (o >> 4) * 8 + (o & 7))

    def first_order(n):
        loads[2 + n].wait()
        sa[n] = dot(to_plane, raw[n].reshape(256, D)).astype(BF).reshape(16, 16, D)

    first_order(0)
    pl.semaphore_wait(barrier, 26)

    def zh_copy(k):
        ref = z.at[zl, zh]
        return copy(ref, ref, zh_s.at[k], zh_r.at[k], at_zh(k))

    ring = (1, -1, 2)

    def zl_copy(n, group):
        ref = z.at[zl, group]
        return copy(ref, ref, zl_s.at[n, group], zl_r.at[n, group], at_ring(ring[n]))

    def zl_arrived(n, group):
        ref = z.at[m4(zl - ring[n]), group]
        copy(ref, ref, zl_s.at[n, group], zl_r.at[n, group], at_ring(ring[n])).wait_recv()

    for k in (2, 1, 3):
        zh_copy(k).start()
    for n in range(3):
        zl_copy(n, zh).start()

    def a_copy(n, k):
        return copy(sa.at[n, m4(x + k // 4) * 4 + m4(y + lax.rem(k, 4))], ra.at[n, xy],
                    a_s.at[n, k], a_r.at[n, k], at_xy(k))

    def a_send(n):
        for k in (10, 8, 2, 9, 11, 6, 14, 5, 7, 13, 15, 4, 12, 1, 3):
            a_copy(n, k).start()

        ra[n, xy] = sa[n, xy]

    a_send(0)
    first_order(1)
    a_send(1)

    for k in (1, 3, 2):
        zh_copy(k).wait_recv()
        for n in range(3):
            zl_copy(n, m4(zh - k)).start()

    def b_copy(n, k):
        return copy(sb.at[n, m4(zl + k)], rb.at[n, zl], b_s.at[n, k], b_r.at[n, k], at_zl(k))

    crossing = 3 - 2 * lax.rem(zl, 2)
    line_order = (2, crossing, 4 - crossing)
    to_line = pick(lambda o: ((o >> 1) & 15) * 16 + ((o >> 5) & 1) * 8 + (o >> 6) * 2 + (o & 1))

    def second_step(n):
        for k in range(1, 16):
            a_copy(n, k).wait()

        sb[n] = dot(to_line, ra[n].reshape(256, D)).astype(BF).reshape(4, 64, D)
        for k in line_order:
            b_copy(n, k).start()
        rb[n, zl] = sb[n, zl]

    mine = zh // 2

    def rows_of(group):
        parts = []
        for k in range(4):
            stored = z[k, group].astype(F32)
            parts.append(stored[:, :640])
            for j in range(2):
                parts.append(jnp.concatenate(
                    [stored[5 * j + m:5 * j + m + 1, 640:768] for m in range(5)], axis=1
                ))
        return jnp.concatenate(parts, axis=0)

    def unit(half):
        for n in range(3):
            for b in range(2):
                zl_arrived(n, 2 * half + b)
        a, b = rows_of(2 * half), rows_of(2 * half + 1)
        return jnp.concatenate([a[:, :432], b[:, :432], a[:, 432:576], b[:, 432:576]], axis=1)

    first_axis = ((c, (1 - c)), ((1 - c), c))

    def shifted(st, i, j):
        fx, fy = first_axis[st]
        return m4(x + i * fx + j * fy), m4(y + i * fy + j * fx)

    def block_of(core, st, px, py):
        return xs.at[core, st, px, py, pl.ds(0, 64)] if st == 0 else xs.at[core, st, px, py]

    def held(st, i, j):
        px, py = shifted(st, i, j)
        return block_of(c, st, px, py)

    sent = []

    def w_send(st, i, j, to_i, to_j):
        ref = held(st, i, j)
        px, py = shifted(st, to_i, to_j)
        index = ((i - to_i) % 4) * 4 + (j - to_j) % 4
        cp = copy(ref, ref, w_s.at[st, index], w_r.at[st, index], dev(px, py, zfull, c))
        cp.start()
        sent.append(cp)

    def w_over(st, i, j):
        ref = held(st, i, j)
        index = i * 4 + j
        cp = copy(ref, ref, wc_s.at[st, index], wc_r.at[st, index], other)
        cp.start()
        sent.append(cp)

    def w_arrived(st, i, j):
        ref = held(st, i, j)
        index = i * 4 + j
        copy(ref, ref, w_s.at[st, index], w_r.at[st, index], other).wait_recv()
        w_over(st, i, j)

    def w_both_ways(st, i):
        w_send(st, i, 0, 0, 1)
        w_send(st, i, 0, 0, -1)

    def w_sides(st, i):
        w_arrived(st, i, 3)
        if i in (0, 2):
            w_send(st, i, 3, 0, 1)
        w_arrived(st, i, 1)
        if i in (1, 3):
            w_send(st, i, 1, 0, -1)

    def w_first(st):
        for i in (1, -1):
            w_send(st, 0, 0, i, 0)
        w_both_ways(st, 0)
        w_over(st, 0, 0)

    second_step(0)
    near = unit(mine)
    xs[c, 0, x, y, 0:64, :] = near[:64].astype(BF)
    w_first(0)
    far = unit(1 - mine)
    xs[c, 1, x, y, 0:64, :] = far[:64].astype(BF)
    xs[c, 1, x, y, 64:80, :] = jnp.concatenate([
        jnp.where(mine == 0, near[64:], far[64:]), jnp.where(mine == 0, far[64:], near[64:])
    ], axis=0).astype(BF)
    w_first(1)
    second_step(1)
    for i in (1, 3):
        for st in range(2):
            w_arrived(st, i, 0)
            if (st, i) in ((0, 3), (1, 1)):
                w_send(st, i, 0, 1 if i == 3 else -1, 0)
            w_both_ways(st, i)
    for st in range(2):
        w_sides(st, 0)
    for st in range(2):
        w_arrived(st, 2, 0)
        w_both_ways(st, 2)

    def places_of(i):
        clip, lines = lax.rem(i, 2), pl.ds(pl.multiple_of(i // 2 * 2, 2), 2)
        rows = pl.ds(pl.multiple_of(clip * 128 + i // 2 * 64, 64), 64)
        return clip, lines, rows, pl.ds(pl.multiple_of(clip * 32, 32), 32)

    def norm_rows(i):
        clip, lines, rows, source = places_of(i)
        tile = rb[0, lines, source, :].reshape(64, D).astype(F32)
        mean = jnp.sum(tile, axis=1, keepdims=True) * (1.0 / D)
        centred = tile - mean
        inv_std = lax.rsqrt(jnp.sum(centred * centred, axis=1, keepdims=True) * (1.0 / D) + EPS)
        nrm = centred * inv_std
        normed[rows, :] = nrm
        inv[rows, :] = jnp.broadcast_to(inv_std, (64, 128))
        hid[rows, :] = (nrm * (1.0 + mod_ref[1, pl.ds(clip, 1), :]) + mod_ref[0, pl.ds(clip, 1), :]).astype(BF)

    def gate_rows(i):
        clip, lines, rows, source = places_of(i)
        cot = rb[1, lines, source, :].reshape(64, D).astype(F32)
        g = (cot * mod_ref[2, pl.ds(clip, 1), :]).astype(BF).astype(F32)
        for core in range(2):
            for half in range(2):
                d = 4 * half + core
                gated[core, half, rows, :] = jnp.concatenate([
                    jnp.zeros((64, 96), F32), g[:, 144 * d:144 * d + 144], g[:, 144 * d + 288:144 * d + 432]
                ], axis=1).astype(BF)

    def hidden_in(places):
        return dot(hid[...], places, RHS_T).astype(BF)

    def table_column(yj):
        return jnp.concatenate(
            [table[pl.ds(pl.multiple_of((k * 4 + yj) * 64, 64), 64), :] for k in range(4)], axis=0
        )

    def table_row(xj):
        return table[pl.ds(pl.multiple_of(xj * 256, 256), 256), :]

    def main_block(core, st, j, cols):
        if core != st:
            return xs[core, st, :, m4(y + j), 0:64, cols].reshape(256, -1)
        return xs[core, st, m4(x + j), :, 0:64, cols].reshape(256, -1)

    def tail_block(core, cols):
        return xs[core, 1, :, :, 64:80, cols].reshape(TAIL, -1)

    units = [(core, st) for core in range(2) for st in range(2)]

    def half_of(st):
        return lax.rem(mine + st, 2)

    def project(j, last=False):
        for core, st in units:
            for cols in (pl.ds(0, 512), pl.ds(512, 384)):
                now = dot(hidg[j, 0 if core != st else 1], main_block(core, st, j, cols))
                if j == 0:
                    acc[core, st, :, cols] = now
                elif not last:
                    acc[core, st, :, cols] += now
                else:
                    tail = dot(hidt[half_of(st)], tail_block(core, cols))
                    pr[core, half_of(st), :, cols] = (acc[core, st, :, cols] + now + tail).astype(BF)

    def by_columns_first(part):
        return jnp.concatenate([
            part[:, (b * 4 + a) * 64:(b * 4 + a) * 64 + 64] for a in range(4) for b in range(4)
        ], axis=1)

    def lanes_of(column, j):
        at = m4(y + j) if column else m4(x + j)
        return pl.ds(pl.multiple_of(at * 256, 256), 256)

    def upright_rows(j):
        for core, st in units:
            xt[core, st, :, lanes_of(core != st, j)] = main_block(core, st, j, pl.ds(0, 896)).T

    out_cols = pl.ds(768, 384)

    def project_grad(j):
        for column in (True, False):
            acc_grad[int(column), :, lanes_of(column, j)] = sum(
                dot(gated[core, half_of(st)], main_block(core, st, j, out_cols), RHS_T)
                for core, st in units if (core != st) == column
            )

    def place_grad():
        main = (acc_grad[0] + by_columns_first(acc_grad[1])).astype(BF)
        first, second = [
            sum(dot(gated[core, half], tail_block(core, out_cols), RHS_T) for core in range(2)) for half in range(2)
        ]
        ends = (first + pltpu.roll(second, TAIL - 8, 1)).astype(BF)
        pr_grad[...] = (dot(main, table[0:MAIN, :]) + dot(ends, table[MAIN:MAIN + TAIL, :])).astype(BF)

    def w_across(i, j):
        for st in range(2):
            px, py = shifted(1 - st, i, j)
            ref = block_of(1 - c, st, px, py)
            index = i * 4 + j
            copy(ref, ref, wc_s.at[st, index], wc_r.at[st, index], other).wait_recv()

    for k in (1, 2, 3):
        b_copy(0, k).wait()
    for load in loads[4:]:
        load.wait()
    pl.loop(0, 4)(norm_rows)
    for k in range(2):
        hidt[k] = hidden_in(table[MAIN + k * TAIL:MAIN + (k + 1) * TAIL, :])
    for j in range(4):
        hidg[j, 0] = hidden_in(table_column(m4(y + j)))
        hidg[j, 1] = hidden_in(table_row(m4(x + j)))
    for st in range(2):
        w_sides(st, 1)
    for i in range(4):
        w_across(i, 0)
    project(0)
    upright_rows(0)
    for i in (3, 2):
        for st in range(2):
            w_sides(st, i)
    for j in (3, 1):
        for i in range(4):
            w_across(i, j)
        project(j)
        upright_rows(j)
    for k in (1, 2, 3):
        b_copy(1, k).wait()
    pl.loop(0, 4)(gate_rows)
    for j in (0, 3, 1):
        project_grad(j)
    for i in range(4):
        for st in range(2):
            w_arrived(st, i, 2)
    for i in range(4):
        w_across(i, 2)
    project(2, last=True)
    project_grad(2)
    place_grad()
    upright_rows(2)
    for cp in sent:
        cp.wait_send()
    for k in (1, 2, 3):
        zh_copy(k).wait_send()
    for n in range(3):
        for k in range(4):
            zl_copy(n, m4(zh - k)).wait_send()

    score_scale = 1.0 / math.sqrt(HD)
    same = (iota((128, 256), 0) & 1) == (iota((128, 256), 1) & 1)

    def attend(clip):
        rows = pl.ds(clip * 128, 128)
        heads_acc[...] = jnp.zeros_like(heads_acc)

        def window_of(pair):
            d = pair // 3
            start = (3 * ((d // 2) % 2) + pair % 3) * 2 * HD
            return (d % 2, d // 4), pl.ds(start // 128 * 128, 256), start % 128

        def move(window, old, new):
            if old == new:
                return window
            return pltpu.roll(window.astype(F32), (new - old) % 256, 1).astype(BF)

        zero = jnp.zeros((128, 256), BF)
        lanes = iota((128, 256), 1)

        def by_head(window, offset):
            lane = lanes - offset
            return jnp.concatenate([
                jnp.where((lane >= 0) & (lane < HD), window, zero),
                jnp.where((lane >= HD) & (lane < 2 * HD), window, zero),
            ], axis=0)

        for i in range(H // 2):
            (qu, q_cols, q_at), (ku, k_cols, k_at), (vu, v_cols, v_at) = [window_of(n * 8 + i) for n in range(3)]
            g_at = i * 2 * HD % 128
            g_cols = pl.ds(i * 2 * HD // 128 * 128, 256)
            keys, values = pr[*ku, rows, k_cols], pr[*vu, rows, v_cols]
            queries = by_head(move(pr[*qu, rows, q_cols], q_at, k_at), k_at)
            grads = by_head(move(pr_grad[rows, g_cols], g_at, v_at), v_at)
            scores = dot(keys, queries, RHS_T) * score_scale
            e = jnp.exp(jnp.where(same, scores, -jnp.inf))
            probs = e * (1.0 / jnp.sum(e, axis=0, keepdims=True))
            grad_probs = dot(values, grads, RHS_T)
            inner = jnp.sum(probs * grad_probs, axis=0, keepdims=True)
            grad_scores = (probs * (grad_probs - inner) * score_scale).astype(BF)
            upright = jnp.concatenate([grad_scores[:, 0:128], grad_scores[:, 128:256]], axis=0)
            heads_acc[*qu, :, q_cols] += dot(upright, by_head(move(keys, k_at, q_at), q_at), LHS_T)
            heads_acc[*ku, :, k_cols] += dot(grad_scores, queries)
            heads_acc[*vu, :, v_cols] += dot(probs.astype(BF), grads)

        gp[...] = heads_acc[...].astype(BF)

    def back_rows(clip):
        by_row, by_column = [
            sum(dot(gp[core, half_of(st)], xt[core, st]) for core, st in units if (core != st) == column)
            for column in (False, True)
        ]
        gh_rows[:, 0:MAIN] = (by_row + by_columns_first(by_column)).astype(BF)
        tails = sum(
            dot(gp[core].reshape(256, 896), tail_block(core, pl.ds(0, 896)), RHS_T) for core in range(2)
        )
        gh_rows[:, MAIN:MAIN + TAIL] = tails[0:128].astype(BF)
        gh_rows[:, MAIN + TAIL:MAIN + 2 * TAIL] = tails[128:256].astype(BF)
        gh[...] = dot(gh_rows[...], table[...])

        shift_sum = jnp.sum(gh[...], axis=0, keepdims=True)
        scale_sum = jnp.sum(gh[...] * normed[clip * 128:clip * 128 + 128, :], axis=0, keepdims=True)
        for n, row in enumerate((shift_sum, scale_sum)):
            n += 2 * clip
            ms[0, n:n + 1, :] = row[:, 0:640]
            ms[0, n + 4:n + 5, 0:512] = row[:, 640:1152]
            ms[0, n + 4:n + 5, 512:640] = jnp.zeros((1, 128), F32)
        if clip == 1:
            m_start(0)

        for part in range(2):
            rows = pl.ds(clip * 128 + part * 64, 64)
            source = pl.ds(clip * 32, 32)
            grad_hidden = gh[part * 64:part * 64 + 64, :]
            nrm = normed[rows, :]
            gn = grad_hidden * (1.0 + mod_ref[1, clip:clip + 1, :])
            mean_grad = jnp.sum(gn, axis=1, keepdims=True) * (1.0 / D)
            mean_cross = jnp.sum(gn * nrm, axis=1, keepdims=True) * (1.0 / D)
            cot = rb[1, 2 * part:2 * part + 2, source, :].reshape(64, D).astype(F32)
            gt = cot + inv[rows, 0:1] * (gn - mean_grad - nrm * mean_cross)
            rr[0, 2 * part:2 * part + 2, source, :] = gt.astype(BF).reshape(2, 32, D)

        for piece in range(2):
            for k in line_order:
                back_copy(clip, piece, k).start()
        rr.at[1, zl][clip * 32:clip * 32 + 32, :] = rr.at[0, zl][clip * 32:clip * 32 + 32, :]

    def back_copy(clip, piece, k):
        part = pl.ds(clip * 32 + piece * 16, 16)
        return copy(rr.at[0, m4(zl + k), part], rr.at[1, zl, part],
                    c_s.at[clip, piece, k], c_r.at[clip, piece, k], at_zl(k))

    def e_copy(clip, k):
        px, py = m4(x + k // 4), m4(y + lax.rem(k, 4))
        return copy(rr2.at[0, clip, px * 4 + py], rr2.at[1, clip, xy],
                    e_s.at[clip, k], e_r.at[clip, k], dev(px, py, zfull, c))

    def line_row(o):
        return ((o >> 1) & 3) * 16 + (o >> 4) * 2 + (o & 1)

    both_halves = pick(lambda o: line_row(o) + ((o >> 3) & 1) * 64, 128, 128)
    top_half = pick(lambda o: jnp.where(((o >> 3) & 1) == 0, line_row(o), -1), 128, 64)

    def plane_start(clip):
        for piece in range(2):
            for k in (1, 2, 3):
                back_copy(clip, piece, k).wait()
            source = pl.ds(clip * 32 + piece * 16, 16)
            to = pl.ds(piece * 8, 8)
            block = rr[1, :, source, :].reshape(64, D)
            stacked = jnp.concatenate([block[:, 0:512], block[:, 640:1152]], axis=0)
            rr2[0, clip, to, :, 0:512] = dot(both_halves, stacked).astype(BF).reshape(8, 16, 512)
            rr2[0, clip, to, :, 512:640] = dot(top_half, block[:, 512:640]).astype(BF).reshape(8, 16, 128)
            for a in range(2):
                i = m4(2 * piece + a - x)
                for j in (2, 1, 3):
                    e_copy(clip, i * 4 + j).start()

                @pl.when(i != 0)
                def _(i=i):
                    e_copy(clip, i * 4).start()

        rr2[1, clip, xy] = rr2[0, clip, xy]

    upper = pick(lambda o: (o >> 3) * 16 + (o & 7), 128, 256)
    lower = pick(lambda o: (o >> 3) * 16 + 8 + (o & 7), 128, 256)

    def finish(clip):
        for k in range(1, 16):
            e_copy(clip, k).wait()

        rows = rr2[1, clip].reshape(256, 640)
        out[clip, :, 0:640] = dot(upper, rows).astype(BF)
        out[clip, :, 640:1152] = dot(lower, rows[:, 0:512]).astype(BF)
        cp = pltpu.make_async_copy(out.at[clip], out_hbm.at[clip], out_sem.at[clip])
        cp.start()
        return cp

    places = (zl, x, y)

    def m_copy(step, k):
        to = (at_zl(k), dev(m4(x + k), y, zfull, c), dev(x, m4(y + k), zfull, c))[step]
        return copy(ms.at[step], mr.at[step, places[step]], m_s.at[step, k], m_r.at[step, k], to)

    def m_start(step):
        for k in (1, 2, 3):
            m_copy(step, k).start()
        mr[step, places[step]] = ms[step]

    def m_sum(step):
        for k in (1, 2, 3):
            m_copy(step, k).wait()
        return ((mr[step, 0] + mr[step, 1]) + mr[step, 2]) + mr[step, 3]

    attend(0)
    back_rows(0)
    attend(1)
    plane_start(0)
    back_rows(1)
    ms[1] = m_sum(0)
    m_start(1)
    stored_first = finish(0)
    ms[2] = m_sum(1)
    m_start(2)
    plane_start(1)
    total = m_sum(2)
    for clip in range(2):
        outm_ref[clip, :, 0:640] = total[2 * clip:2 * clip + 2]
        outm_ref[clip, :, 640:1152] = total[4 + 2 * clip:6 + 2 * clip, 0:512]
    stored_second = finish(1)
    stored_first.wait()
    stored_second.wait()


def local(tokens, modulation, cotangent, qkv_weight, out_weight):
    table = jnp.asarray(place_table(), BF)
    hbm = pl.BlockSpec(memory_space=pl.ANY)
    dma = pltpu.SemaphoreType.DMA
    vmem = pltpu.VMEM
    grad_tokens, grad_modulation = pl.pallas_call(
        kernel,
        out_shape=(
            jax.ShapeDtypeStruct((2, 128, D), BF),
            jax.ShapeDtypeStruct((2, 2, D), F32),
        ),
        in_specs=[hbm] * 6,
        out_specs=(hbm, pl.BlockSpec(memory_space=pltpu.VMEM)),
        scratch_shapes=[
            vmem((2, 2, 128, D), BF),
            vmem((3, 2, D), F32),
            vmem((18, 432), BF),
            vmem((18, 144), BF),
            vmem((2, 16, 16, D), BF),
            vmem((2, 16, 16, D), BF),
            vmem((2, 4, 64, D), BF),
            vmem((2, 4, 64, D), BF),
            vmem((4, 4, 16, 768), BF),
            vmem((2, 2, 4, 4, 80, D), BF),
            vmem((2, 2, 896, MAIN), BF),
            vmem((MAIN + 2 * TAIL, D), BF),
            vmem((256, D), BF),
            vmem((4, 2, 256, 256), BF),
            vmem((2, 256, TAIL), BF),
            vmem((2, 2, 256, 384), BF),
            vmem((256, D), F32),
            vmem((256, 128), F32),
            vmem((2, 2, 256, 896), F32),
            vmem((2, 256, MAIN), F32),
            vmem((2, 2, 256, 896), BF),
            vmem((256, D), BF),
            vmem((2, 2, 128, 896), F32),
            vmem((2, 2, 128, 896), BF),
            vmem((128, MAIN + 2 * TAIL), BF),
            vmem((128, D), F32),
            vmem((2, 4, 64, D), BF),
            vmem((2, 2, 16, 16, 640), BF),
            vmem((2, 128, D), BF),
            vmem((3, 8, 640), F32),
            vmem((3, 4, 8, 640), F32),
            dma((6,)), dma((2,)),
            dma((4,)), dma((4,)), dma((3, 4)), dma((3, 4)),
            dma((2, 16)), dma((2, 16)), dma((2, 16)), dma((2, 16)),
            dma((2, 16)), dma((2, 16)), dma((2, 4)), dma((2, 4)),
            dma((2, 2, 4)), dma((2, 2, 4)), dma((2, 16)), dma((2, 16)),
            dma((3, 4)), dma((3, 4)),
        ],
        compiler_params=pltpu.CompilerParams(
            collective_id=0, has_side_effects=True, vmem_limit_bytes=60 * 1024 * 1024
        ),
        name="sublayer_backward",
    )(
        tokens.reshape(2, 128, D), modulation.transpose(1, 0, 2), cotangent.reshape(2, 128, D),
        qkv_weight, out_weight, table,
    )
    return grad_tokens.reshape(2, 1, 128, D), grad_modulation


def solution(mesh):
    in_specs = (
        P("dp", "seq", None, None),
        P("dp", None, None),
        P("dp", "seq", None, None),
        P("seq", "dp"),
        P("seq", "dp"),
    )
    out_specs = (P("dp", "seq", None, None), P("dp", None, None))
    return jax.shard_map(local, mesh=mesh, in_specs=in_specs, out_specs=out_specs, check_vma=False)
```
